128 devices in a mesh: seq: 16 (over y, x), mp: 4 (over z), section: 2 (over core).
Axes of the slice: x: 4, y: 4, z: 4, core: 2. Of those that a mesh axis runs over, the one named last changes fastest.
Arguments:
- out_grad: bfloat16 [8192, 4608], P('seq', ('mp', 'section')), may hold values from -6 to 6
- out_weight: bfloat16 [4096, 4608], P(None, ('mp', 'section')), may hold values from -0.09375 to 0.09375
- query_states: bfloat16 [8192, 4096], P('seq', ('mp', 'section')), may hold values from -6 to 6
- key_states: bfloat16 [8192, 2048], P('seq', ('mp', 'section')), may hold values from -6 to 6
- value_states: bfloat16 [8192, 2048], P('seq', ('mp', 'section')), may hold values from -6 to 6
- slot_seq: int32 [128], replicated, may hold values from 0 to 16, as said below
- slot_pos: int32 [128], replicated, may hold values from 0 to 15, as said below
- fork_depth: int32 [16], replicated, may hold values from 1 to 16, as said below
Outputs:
- query_grad: bfloat16 [8192, 4096], P('seq', ('mp', 'section'))
- key_grad: bfloat16 [8192, 2048], P('seq', ('mp', 'section'))
- value_grad: bfloat16 [8192, 2048], P('seq', ('mp', 'section'))
The draws below stay inside these ranges and needn't reach their ends.
Inputs may be any that keep to these rules, and one draw needn't show every extreme that they name: `slot_seq`: blocks are listed device by device, 8 to a device along seq. Every device holds all blocks of exactly one response and fills its other slots with prompt blocks, at most 2 of them and exactly 2 on some device; as many devices hold 2 prompt blocks as hold none. Each of the 16 responses and each of the 16 prompt blocks appears once. Slots are in no particular order. `slot_pos`: prompt blocks carry indices 0 to 15; a response's blocks are numbered from 0 without gaps. `fork_depth`: some response sees the whole prompt and some other response only its first block.
All inputs are finite; a program needn't handle non-finite values.
Results may differ from the reference program's by a relative error of at most 0.017.
Values may be sent and summed in bfloat16 or wider, within the bound.
No kernel may reach another device: no remote copies, remote signals or barrier semaphores. Data moves between devices by JAX's collectives and lax.ppermute only.
A program may use at most 128 MiB of HBM per device.

```python
import jax
import jax.numpy as jnp
from jax import lax

D = 4608
HQ = 32
HK = 16
HD = 128
BLK = 64
BLK_DEV = 8
TOKENS = 8192
N_SEQ = 16


def tree_layout(key):
    devices = N_SEQ
    keys_list = jax.random.split(key, 7)
    order = jax.random.permutation(keys_list[0], devices)
    coin = jax.random.randint(keys_list[1], (devices // 2,), 0, 2)
    coin = jnp.where(jnp.arange(devices // 2) == 0, 1, coin)
    first = jnp.where(coin == 1, 2, 1)
    second = 2 - first
    ordered = jnp.stack([first, second], axis=1).reshape(-1)
    counts = jnp.zeros((devices,), jnp.int32).at[order].set(ordered.astype(jnp.int32))
    ranks = jax.vmap(lambda sub: jax.random.permutation(sub, BLK_DEV))(jax.random.split(keys_list[2], devices))
    ranks = ranks.astype(jnp.int32)
    is_prompt = ranks < counts[:, None]
    prefix = jnp.cumsum(counts) - counts
    global_index = jnp.clip(prefix[:, None] + ranks, 0, devices - 1)
    prompt_perm = jax.random.permutation(keys_list[3], devices).astype(jnp.int32)
    prompt_pos = prompt_perm[global_index]
    branch_of = jax.random.permutation(keys_list[4], devices).astype(jnp.int32)
    slot_seq = jnp.where(is_prompt, 0, 1 + branch_of[:, None])
    slot_pos = jnp.where(is_prompt, prompt_pos, ranks - counts[:, None])
    fork = jax.random.randint(keys_list[5], (devices,), 1, devices + 1)
    chosen = jax.random.randint(keys_list[6], (), 0, devices)
    other = (chosen + 1) % devices
    index = jnp.arange(devices)
    fork = jnp.where(index == other, 1, fork)
    fork = jnp.where(index == chosen, devices, fork)
    return (slot_seq.reshape(-1).astype(jnp.int32), slot_pos.reshape(-1).astype(jnp.int32), fork.astype(jnp.int32))


def draw_slot_seq(key, part):
    return tree_layout(key)[0]


def draw_slot_pos(key, part):
    return tree_layout(key)[1]


def draw_fork_depth(key, part):
    return tree_layout(key)[2]


def block_scale(key, extent, cuts, low, high):
    factor_of = 1.0
    for axis_at, blocks in cuts:
        heights = jax.random.uniform(jax.random.fold_in(jax.random.fold_in(key, 6), axis_at), (blocks,), jnp.float32, low / len(cuts), high / len(cuts))
        factor_of = factor_of * jnp.repeat(jnp.exp(heights), extent[axis_at] // blocks).reshape((-1,) + (1,) * (len(extent) - 1 - axis_at))
    return factor_of


def noise(key, dims, scale, reach, shards=(), held_as=jnp.bfloat16):
    factor_of = block_scale(key, dims, shards, -0.22, 0.18) if shards else 1.0
    drawn = jax.random.normal(key, dims, jnp.float32) * scale * factor_of
    return jnp.minimum(jnp.maximum(drawn, -reach), reach).astype(held_as)


def setup_inputs(seed: int = 0) -> dict:
    key_list = jax.random.split(jax.random.key(seed), 9)
    return {
        "out_grad": noise(key_list[0], (TOKENS, D), 1.0, 6.0, ((0, 16), (1, 8))),
        "out_weight": noise(key_list[1], (HQ * HD, D), D ** -0.5, 0.09375, ((1, 8),)),
        "query_states": noise(key_list[2], (TOKENS, HQ * HD), 1.0, 6.0, ((0, 16), (1, 8))),
        "key_states": noise(key_list[3], (TOKENS, HK * HD), 1.0, 6.0, ((0, 16), (1, 8))),
        "value_states": noise(key_list[4], (TOKENS, HK * HD), 1.0, 6.0, ((0, 16), (1, 8))),
        "slot_seq": draw_slot_seq(jax.random.fold_in(key_list[8], 71), 0),
        "slot_pos": draw_slot_pos(jax.random.fold_in(key_list[8], 71), 0),
        "fork_depth": draw_fork_depth(jax.random.fold_in(key_list[8], 71), 0),
    }


SCALE = 144.0 ** -0.5
SOFTCAP = 50.0


def token_meta(slot_seq, slot_pos, fork_depth):
    offset = jnp.arange(BLK, dtype=jnp.int32)
    seq_tok = jnp.repeat(slot_seq, BLK)
    pos_tok = (slot_pos[:, None] * BLK + offset[None, :]).reshape(-1)
    branch = jnp.arange(fork_depth.shape[0], dtype=jnp.int32) + 1
    table = (seq_tok[:, None] == branch[None, :]).astype(jnp.int32)
    depth_tok = jnp.sum(table * fork_depth[None, :], axis=1) * BLK
    return seq_tok, pos_tok, depth_tok


def allowed(qseq, qpos, qdepth, kseq, kpos):
    qs = qseq[:, None]
    qp = qpos[:, None]
    ks = kseq[None, :]
    kp = kpos[None, :]
    prompt_key = jnp.where(qs == 0, kp <= qp, kp < qdepth[:, None])
    own_key = (ks == qs) & (kp <= qp)
    return jnp.where(ks == 0, prompt_key, own_key)


def attend(qblock, gblock, keys_f, values_f, mask):
    qf = qblock.astype(jnp.float32)
    gf = gblock.astype(jnp.float32)
    raw = jnp.einsum('ngd,md->gnm', qf, keys_f) * SCALE
    tanh_val = jnp.tanh(raw / SOFTCAP)
    expo = jnp.where(mask[None], jnp.exp(SOFTCAP * tanh_val), 0.0)
    dprob = jnp.einsum('ngd,md->gnm', gf, values_f)
    total = jnp.sum(expo, axis=-1)
    delta = jnp.sum(expo * dprob, axis=-1) / total
    prob = expo / total[..., None]
    dscore = prob * (dprob - delta[..., None]) * (1.0 - tanh_val * tanh_val) * SCALE
    prob16 = lax.optimization_barrier(prob.astype(jnp.bfloat16)).astype(jnp.float32)
    dscore16 = lax.optimization_barrier(dscore.astype(jnp.bfloat16)).astype(jnp.float32)
    dquery = jnp.einsum('gnm,md->ngd', dscore16, keys_f)
    dkey = jnp.einsum('gnm,ngd->md', dscore16, qf)
    dvalue = jnp.einsum('gnm,ngd->md', prob16, gf)
    return dquery, dkey, dvalue


def reference(out_grad, out_weight, query_states, key_states, value_states, slot_seq, slot_pos, fork_depth):
    head_grad = lax.dot_general(out_grad, out_weight, (((1,), (1,)), ((), ())),
                                preferred_element_type=jnp.float32).astype(jnp.bfloat16)
    seq_tok, pos_tok, depth_tok = token_meta(slot_seq, slot_pos, fork_depth)
    tokens = query_states.shape[0]
    group = HQ // HK
    qblk = 512 if tokens % 512 == 0 else tokens
    nblk = tokens // qblk

    def per_head(head):
        qh = lax.dynamic_slice_in_dim(query_states, head * group * HD, group * HD, 1).reshape(tokens, group, HD)
        gh = lax.dynamic_slice_in_dim(head_grad, head * group * HD, group * HD, 1).reshape(tokens, group, HD)
        keys_f = lax.dynamic_slice_in_dim(key_states, head * HD, HD, 1).astype(jnp.float32)
        values_f = lax.dynamic_slice_in_dim(value_states, head * HD, HD, 1).astype(jnp.float32)

        def step(carry, index):
            dkey_acc, dvalue_acc = carry
            start = index * qblk
            qblock = lax.dynamic_slice_in_dim(qh, start, qblk, 0)
            gblock = lax.dynamic_slice_in_dim(gh, start, qblk, 0)
            mask = allowed(lax.dynamic_slice_in_dim(seq_tok, start, qblk, 0),
                           lax.dynamic_slice_in_dim(pos_tok, start, qblk, 0),
                           lax.dynamic_slice_in_dim(depth_tok, start, qblk, 0),
                           seq_tok, pos_tok)
            dquery, dkey, dvalue = attend(qblock, gblock, keys_f, values_f, mask)
            return (dkey_acc + dkey, dvalue_acc + dvalue), dquery

        zeros = jnp.zeros((tokens, HD), jnp.float32)
        (dkey, dvalue), dquery = lax.scan(step, (zeros, zeros), jnp.arange(nblk, dtype=jnp.int32))
        return dquery.reshape(tokens, group * HD), dkey, dvalue

    dquery, dkey, dvalue = lax.map(per_head, jnp.arange(HK, dtype=jnp.int32))
    query_grad = jnp.transpose(dquery, (1, 0, 2)).reshape(tokens, HQ * HD).astype(jnp.bfloat16)
    key_grad = jnp.transpose(dkey, (1, 0, 2)).reshape(tokens, HK * HD).astype(jnp.bfloat16)
    value_grad = jnp.transpose(dvalue, (1, 0, 2)).reshape(tokens, HK * HD).astype(jnp.bfloat16)
    return query_grad, key_grad, value_grad
```

```python
import functools

import jax
import jax.numpy as jnp
from jax import lax
from jax.experimental import pallas as pl
from jax.experimental.pallas import tpu as pltpu
from jax.sharding import PartitionSpec as P

HD = 128
BLK = 64
BLK_DEV = 8
PCAP = 2
ROWS = BLK * BLK_DEV
PKEYS = 16 * BLK
KEYS = PKEYS + ROWS
CHUNK = 256
QB = 256

SCALE = 144.0 ** (-0.5)
SOFTCAP = 50.0

INV = 0
ORDER = 32
BASE = 40
RESP = 48
COUNT = 56
META = 64

SMEM = pltpu.MemorySpace.SMEM
VMEM = pltpu.MemorySpace.VMEM


def params(mib):
    return pltpu.CompilerParams(vmem_limit_bytes=mib * 2**20)


def layout_kernel(ids, seq, pos, depth, keys, values, meta, out):
    me = ids[0]
    for i in range(META):
        meta[i] = jnp.int32(-1)

    def device(dev, carry):
        count = jnp.int32(0)
        for b in range(BLK_DEV):
            slot = dev * BLK_DEV + b
            prompt = seq[slot] == 0

            @pl.when(prompt)
            def _(count=count, slot=slot):
                meta[INV + dev * PCAP + jnp.minimum(count, PCAP - 1)] = pos[slot]

            count = count + prompt.astype(jnp.int32)
        return carry

    lax.fori_loop(0, 16, device, 0)
    count = jnp.int32(0)
    for b in range(BLK_DEV):
        slot = me * BLK_DEV + b
        prompt = seq[slot] == 0
        at = jnp.where(prompt, BLK_DEV - 1 - count, pos[slot])
        meta[ORDER + at] = jnp.int32(b)
        meta[RESP + at] = 1 - prompt.astype(jnp.int32)
        meta[BASE + at] = jnp.where(prompt, pos[slot], depth[jnp.maximum(seq[slot] - 1, 0)]) * BLK

        @pl.when(prompt)
        def _(count=count, b=b):
            rows = pl.ds(pl.multiple_of(jnp.minimum(count, PCAP - 1) * BLK, BLK), BLK)
            out[0, rows, : keys.shape[1]] = keys[b * BLK : (b + 1) * BLK, :]
            out[0, rows, keys.shape[1] :] = values[b * BLK : (b + 1) * BLK, :]

        count = count + prompt.astype(jnp.int32)
    meta[COUNT] = count
    for b in range(PCAP):

        @pl.when(count <= b)
        def _(b=b):
            out[0, b * BLK : (b + 1) * BLK, :] = jnp.zeros((BLK, out.shape[2]), out.dtype)

    for d in range(1, 16):
        out[d] = out[0]


def layout(ids, slot_seq, slot_pos, fork_depth, keys, values):
    feat = keys.shape[1] + values.shape[1]
    return pl.pallas_call(
        layout_kernel,
        out_shape=(
            jax.ShapeDtypeStruct((META,), jnp.int32),
            jax.ShapeDtypeStruct((16, PCAP * BLK, feat), jnp.bfloat16),
        ),
        in_specs=[pl.BlockSpec(memory_space=SMEM)] * 4 + [pl.BlockSpec(memory_space=VMEM)] * 2,
        out_specs=(pl.BlockSpec(memory_space=SMEM), pl.BlockSpec(memory_space=VMEM)),
        compiler_params=params(16),
        name="layout",
    )(ids, slot_seq, slot_pos, fork_depth, keys, values)


NT = (((1,), (1,)), ((), ()))


def project_peer_kernel(ids, grad, weight, out):
    out[0] = lax.dot_general(grad[...], weight[...], NT, preferred_element_type=jnp.float32).astype(jnp.bfloat16)


def target(ids, r):
    z = ids[1]
    return jnp.where(r == 0, (3 - z) ^ 1, jnp.where(r == 1, z ^ 1, jnp.where(r == 2, 3 - z, z)))


def project_peer(ids, out_grad, out_weight):
    rows, depth = out_grad.shape
    cols = out_weight.shape[0] // 8
    return pl.pallas_call(
        project_peer_kernel,
        out_shape=jax.ShapeDtypeStruct((4, rows, cols), jnp.bfloat16),
        grid_spec=pltpu.PrefetchScalarGridSpec(
            num_scalar_prefetch=1,
            grid=(4,),
            in_specs=[
                pl.BlockSpec((rows, depth), lambda r, ids: (0, 0)),
                pl.BlockSpec((cols, depth), lambda r, ids: (target(ids, r) * 2 + 1 - ids[2], 0)),
            ],
            out_specs=pl.BlockSpec((1, rows, cols), lambda r, ids: (r, 0, 0)),
        ),
        compiler_params=params(32),
        cost_estimate=pl.CostEstimate(flops=4 * 2 * rows * cols * depth, bytes_accessed=5 * 2**20, transcendentals=0),
        name="project_peer",
    )(ids, out_grad, out_weight)


def project_own_kernel(ids, grad, weight, peer, send_a, keep_a, send_b, keep_b):
    r = pl.program_id(0)
    both = lax.dot_general(grad[...], weight[...], NT, preferred_element_type=jnp.float32)
    both = (both + peer[0].astype(jnp.float32)).astype(jnp.bfloat16)
    half = both.shape[1] // 2
    first, second = both[:, :half], both[:, half:]

    @pl.when(r < 2)
    def _():
        send_a[0] = first

    @pl.when(r >= 2)
    def _():
        keep_a[0] = first

    @pl.when(r % 2 == 0)
    def _():
        send_b[0] = second

    @pl.when(r % 2 == 1)
    def _():
        keep_b[0] = second


def project_own(ids, out_grad, out_weight, peer):
    rows, depth = out_grad.shape
    cols = out_weight.shape[0] // 8
    part = jax.ShapeDtypeStruct((2, rows, cols // 2), jnp.bfloat16)

    def at(index):
        return pl.BlockSpec((1, rows, cols // 2), lambda r, ids: (index(r), 0, 0))

    return pl.pallas_call(
        project_own_kernel,
        out_shape=(part, part, part, part),
        grid_spec=pltpu.PrefetchScalarGridSpec(
            num_scalar_prefetch=1,
            grid=(4,),
            in_specs=[
                pl.BlockSpec((rows, depth), lambda r, ids: (0, 0)),
                pl.BlockSpec((cols, depth), lambda r, ids: (target(ids, r) * 2 + ids[2], 0)),
                pl.BlockSpec((1, rows, cols), lambda r, ids: (r, 0, 0)),
            ],
            out_specs=(
                at(lambda r: jnp.where(r == 0, 1, 0)),
                at(lambda r: jnp.where(r == 3, 0, 1)),
                at(lambda r: jnp.where(r == 0, 1, 0)),
                at(lambda r: jnp.where(r >= 2, 0, 1)),
            ),
        ),
        compiler_params=params(32),
        cost_estimate=pl.CostEstimate(flops=4 * 2 * rows * cols * depth, bytes_accessed=7 * 2**20, transcendentals=0),
        name="project_own",
    )(ids, out_grad, out_weight, peer)


def attend_kernel(
    meta, q, k, v, pk, pv, ka, ra, sa, kb, rb, sb,
    dq, dk, dv, ret,
    kc, vc, kt, qc, gc, gsum, dkc, dvc, ex, fx, dp,
):
    a = pl.program_id(0)

    @pl.when(a == 0)
    def _():
        total = ka[0].astype(jnp.float32) + ra[0].astype(jnp.float32) + sa[...].astype(jnp.float32)
        gsum[...] = total.astype(jnp.bfloat16)

    @pl.when(a == 1)
    def _():
        total = kb[0].astype(jnp.float32) + rb[0].astype(jnp.float32) + sb[...].astype(jnp.float32)
        gsum[...] = total.astype(jnp.bfloat16)

    def block(i):
        return pl.ds(pl.multiple_of(i * BLK, BLK), BLK)

    for s in range(32):
        p = meta[INV + s]

        @pl.when(p >= 0)
        def _(s=s, p=p):
            kc[block(p), :] = pk[s * BLK : (s + 1) * BLK, :]
            vc[block(p), :] = pv[s * BLK : (s + 1) * BLK, :]

    lane = lax.broadcasted_iota(jnp.int32, (8, ROWS), 1)
    plim = jnp.zeros((8, ROWS), jnp.int32)
    llim = jnp.zeros((8, ROWS), jnp.int32)
    for j in range(BLK_DEV):
        src = block(meta[ORDER + j])
        kc[PKEYS + j * BLK : PKEYS + (j + 1) * BLK, :] = k[src, :]
        vc[PKEYS + j * BLK : PKEYS + (j + 1) * BLK, :] = v[src, :]
        for h in range(2):
            to = slice(h * ROWS + j * BLK, h * ROWS + (j + 1) * BLK)
            qc[to, :] = q[src, h * HD : (h + 1) * HD]
            gc[to, :] = gsum[src, h * HD : (h + 1) * HD]
        here = (lane >= j * BLK) & (lane < (j + 1) * BLK)
        resp = meta[RESP + j]
        step = lane - (j * BLK - 1)
        plim = jnp.where(here, meta[BASE + j] + step * (1 - resp), plim)
        llim = jnp.where(here, (j * BLK + step) * resp, llim)
    kt[...] = kc[...].T
    sub = lax.broadcasted_iota(jnp.int32, (CHUNK, QB), 0)

    for h in range(2):
        for half in range(ROWS // QB):
            rows = slice(h * ROWS + half * QB, h * ROWS + (half + 1) * QB)
            qb = qc[rows, :]
            gb = gc[rows, :]
            lanes = slice(half * QB, (half + 1) * QB)
            pl_row = plim[:1, lanes]
            ll_row = llim[:1, lanes]
            chunks = PKEYS // CHUNK + half + 1
            total = jnp.zeros((1, QB), jnp.float32)
            weighted = jnp.zeros((1, QB), jnp.float32)
            for c in range(chunks):
                cut = slice(c * CHUNK, (c + 1) * CHUNK)
                raw = lax.dot_general(kc[cut, :], qb, NT, preferred_element_type=jnp.float32)
                dprob = lax.dot_general(vc[cut, :], gb, NT, preferred_element_type=jnp.float32)
                tanh_val = jnp.tanh(raw * (SCALE / SOFTCAP))
                if c * CHUNK < PKEYS:
                    seen = sub < pl_row - c * CHUNK
                else:
                    seen = sub < ll_row - (c * CHUNK - PKEYS)
                expo = jnp.where(seen, jnp.exp(SOFTCAP * tanh_val), 0.0)
                total = total + jnp.sum(expo, axis=0, keepdims=True)
                weighted = weighted + jnp.sum(expo * dprob, axis=0, keepdims=True)
                ex[cut, :] = expo
                fx[cut, :] = expo * (1.0 - tanh_val * tanh_val)
                dp[cut, :] = dprob
            inv = 1.0 / total
            delta = weighted * inv
            scaled = inv * SCALE
            dq_t = jnp.zeros((HD, QB), jnp.float32)
            for c in range(chunks):
                cut = slice(c * CHUNK, (c + 1) * CHUNK)
                prob16 = (ex[cut, :] * inv).astype(jnp.bfloat16)
                dscore16 = (fx[cut, :] * ((dp[cut, :] - delta) * scaled)).astype(jnp.bfloat16)
                dv_part = jnp.dot(prob16, gb, preferred_element_type=jnp.float32)
                dk_part = jnp.dot(dscore16, qb, preferred_element_type=jnp.float32)
                dq_t = dq_t + jnp.dot(kt[:, cut], dscore16, preferred_element_type=jnp.float32)
                first = h == 0 and (half == 0 or c == PKEYS // CHUNK + 1)
                if first:
                    dvc[cut, :] = dv_part
                    dkc[cut, :] = dk_part
                else:
                    dvc[cut, :] += dv_part
                    dkc[cut, :] += dk_part
            dq_rows = dq_t.T.astype(jnp.bfloat16)
            for j in range(QB // BLK):
                dst = block(meta[ORDER + half * (QB // BLK) + j])
                dq[dst, h * HD : (h + 1) * HD] = dq_rows[j * BLK : (j + 1) * BLK, :]

    for j in range(BLK_DEV):
        dst = block(meta[ORDER + j])
        src = slice(PKEYS + j * BLK, PKEYS + (j + 1) * BLK)
        dk[dst, :] = dkc[src, :].astype(jnp.bfloat16)
        dv[dst, :] = dvc[src, :].astype(jnp.bfloat16)
    for s in range(32):
        p = meta[INV + s]
        to = slice((s % 2) * BLK, (s % 2 + 1) * BLK)

        @pl.when(p >= 0)
        def _(s=s, p=p, to=to):
            ret[s // 2, to, :HD] = dkc[block(p), :].astype(jnp.bfloat16)
            ret[s // 2, to, HD:] = dvc[block(p), :].astype(jnp.bfloat16)

        @pl.when(p < 0)
        def _(s=s, to=to):
            ret[s // 2, to, :] = jnp.zeros((BLK, 2 * HD), jnp.bfloat16)


def attend(meta, queries, keys, values, gathered, parts):
    full = pl.BlockSpec((ROWS, 2 * HD), lambda a: (0, 0))
    first = pl.BlockSpec((1, ROWS, 2 * HD), lambda a: (0, 0, 0))
    wide = pl.BlockSpec((ROWS, 2 * HD), lambda a: (0, a))
    narrow = pl.BlockSpec((ROWS, HD), lambda a: (0, a))
    slots = 16 * PCAP * BLK
    return pl.pallas_call(
        attend_kernel,
        out_shape=(
            jax.ShapeDtypeStruct(queries.shape, jnp.bfloat16),
            jax.ShapeDtypeStruct(keys.shape, jnp.bfloat16),
            jax.ShapeDtypeStruct(values.shape, jnp.bfloat16),
            jax.ShapeDtypeStruct((16, PCAP * BLK, 4 * HD), jnp.bfloat16),
        ),
        grid=(2,),
        in_specs=[
            pl.BlockSpec(memory_space=SMEM),
            wide,
            narrow,
            narrow,
            pl.BlockSpec((slots, HD), lambda a: (0, a)),
            pl.BlockSpec((slots, HD), lambda a: (0, 2 + a)),
            first, first, full, first, first, full,
        ],
        out_specs=(wide, narrow, narrow, pl.BlockSpec((16, PCAP * BLK, 2 * HD), lambda a: (0, 0, a))),
        scratch_shapes=[
            pltpu.VMEM((KEYS, HD), jnp.bfloat16),
            pltpu.VMEM((KEYS, HD), jnp.bfloat16),
            pltpu.VMEM((HD, KEYS), jnp.bfloat16),
            pltpu.VMEM((2 * ROWS, HD), jnp.bfloat16),
            pltpu.VMEM((2 * ROWS, HD), jnp.bfloat16),
            pltpu.VMEM((ROWS, 2 * HD), jnp.bfloat16),
            pltpu.VMEM((KEYS, HD), jnp.float32),
            pltpu.VMEM((KEYS, HD), jnp.float32),
            pltpu.VMEM((KEYS, QB), jnp.float32),
            pltpu.VMEM((KEYS, QB), jnp.float32),
            pltpu.VMEM((KEYS, QB), jnp.float32),
        ],
        compiler_params=params(48),
        cost_estimate=pl.CostEstimate(flops=4 * 10**9, bytes_accessed=8 * 2**20, transcendentals=6 * 10**6),
        name="attend",
    )(meta, queries, keys, values, gathered, gathered, *parts)


def finish_kernel(meta, ret, dk_in, dv_in, dk, dv):
    dk[...] = dk_in[...]
    dv[...] = dv_in[...]
    for r in range(PCAP):

        @pl.when(meta[COUNT] > r)
        def _(r=r):
            rows = slice(r * BLK, (r + 1) * BLK)
            at = pl.ds(pl.multiple_of(meta[ORDER + BLK_DEV - 1 - r] * BLK, BLK), BLK)
            for a in range(2):
                for i, out in enumerate((dk, dv)):
                    cols = slice((2 * a + i) * HD, (2 * a + i + 1) * HD)
                    total = ret[0, rows, cols].astype(jnp.float32)
                    for d in range(1, 16):
                        total = total + ret[d, rows, cols].astype(jnp.float32)
                    out[at, a * HD : (a + 1) * HD] = total.astype(jnp.bfloat16)


def finish(meta, ret, dk, dv):
    return pl.pallas_call(
        finish_kernel,
        out_shape=(jax.ShapeDtypeStruct(dk.shape, dk.dtype), jax.ShapeDtypeStruct(dv.shape, dv.dtype)),
        in_specs=[pl.BlockSpec(memory_space=SMEM)] + [pl.BlockSpec(memory_space=VMEM)] * 3,
        out_specs=(pl.BlockSpec(memory_space=VMEM), pl.BlockSpec(memory_space=VMEM)),
        compiler_params=params(16),
        name="finish",
    )(meta, ret, dk, dv)


def shards(out_grad, out_weight, query_states, key_states, value_states, slot_seq, slot_pos, fork_depth):
    ids = jnp.stack([lax.axis_index("seq"), lax.axis_index("mp"), lax.axis_index("section")]).astype(jnp.int32)
    pair_a = [(z, z ^ 1) for z in range(4)]
    pair_b = [(z, 3 - z) for z in range(4)]
    swap = [(0, 1), (1, 0)]

    peer = project_peer(ids, out_grad, out_weight)
    peer = lax.ppermute(peer, "section", swap)
    meta, prompt = layout(ids, slot_seq, slot_pos, fork_depth, key_states, value_states)
    gathered = lax.all_to_all(prompt, "seq", 0, 0, tiled=True).reshape(16 * PCAP * BLK, -1)
    send_a, keep_a, send_b, keep_b = project_own(ids, out_grad, out_weight, peer)
    recv_a = lax.ppermute(send_a, "mp", pair_a)
    recv_b = lax.ppermute(send_b, "mp", pair_b)
    next_a = (keep_a[1].astype(jnp.float32) + recv_a[1].astype(jnp.float32)).astype(jnp.bfloat16)
    next_b = (keep_b[1].astype(jnp.float32) + recv_b[1].astype(jnp.float32)).astype(jnp.bfloat16)
    last_a = lax.ppermute(next_a, "mp", pair_b)
    last_b = lax.ppermute(next_b, "mp", pair_a)
    parts = (keep_a, recv_a, last_a, keep_b, recv_b, last_b)
    dq, dk, dv, ret = attend(meta, query_states, key_states, value_states, gathered, parts)
    ret = lax.all_to_all(ret, "seq", 0, 0, tiled=True)
    dk, dv = finish(meta, ret, dk, dv)
    return dq, dk, dv


def solution(mesh):
    wide = P("seq", ("mp", "section"))
    return jax.shard_map(
        shards,
        mesh=mesh,
        in_specs=(wide, P(None, ("mp", "section")), wide, wide, wide, P(), P(), P()),
        out_specs=(wide, wide, wide),
        check_vma=False,
    )
```

```python
import jax
import jax.numpy as jnp
from jax import lax
from jax.experimental import pallas as pl
from jax.experimental.pallas import tpu as pltpu
from jax.sharding import PartitionSpec as P

HD = 128
BLK = 64
BLK_DEV = 8
PCAP = 2
DEVS = 16
ROWS = BLK * BLK_DEV
PKEYS = 16 * BLK
KEYS = PKEYS + ROWS
CHUNK = 256

SCALE = 144.0 ** (-0.5)
SOFTCAP = 50.0

PLIST = 0
ORDER = 16
BASE = 24
RESP = 32
COUNT = 40
META = 48

LIM = 60

SMEM = pltpu.MemorySpace.SMEM
VMEM = pltpu.MemorySpace.VMEM
NT = (((1,), (1,)), ((), ()))
TN = (((0,), (0,)), ((), ()))


def params(mib):
    return pltpu.CompilerParams(vmem_limit_bytes=mib * 2**20)


def specs(space, n):
    return [pl.BlockSpec(memory_space=space)] * n


def rows_at(i):
    return pl.ds(pl.multiple_of(i * BLK, BLK), BLK)


def place(slot):
    return lax.shift_right_logical(slot, 1), rows_at(slot & 1)


def make_layout(here, seq, pos, depth, keys, values, meta, block):
    me = here[0]

    def device(dev, carry):
        count = jnp.int32(0)
        for b in range(BLK_DEV):
            slot = dev * BLK_DEV + b
            prompt = seq[slot] == 0

            @pl.when(prompt)
            def _(count=count, slot=slot):
                meta[PLIST + pos[slot]] = dev * PCAP + jnp.minimum(count, PCAP - 1)

            count = count + prompt.astype(jnp.int32)
        return carry

    lax.fori_loop(0, DEVS, device, 0)
    count = jnp.int32(0)
    block[...] = jnp.zeros(block.shape, block.dtype)
    for b in range(BLK_DEV):
        slot = me * BLK_DEV + b
        prompt = seq[slot] == 0
        at = jnp.where(prompt, BLK_DEV - 1 - count, pos[slot])
        meta[ORDER + at] = jnp.int32(b)
        meta[RESP + at] = 1 - prompt.astype(jnp.int32)
        meta[BASE + at] = jnp.where(prompt, pos[slot], depth[jnp.maximum(seq[slot] - 1, 0)]) * BLK

        @pl.when(prompt)
        def _(count=count, b=b):
            rows = rows_at(jnp.minimum(count, PCAP - 1))
            for a in range(2):
                block[a, rows, :HD] = keys[b * BLK : (b + 1) * BLK, a * HD : (a + 1) * HD]
                block[a, rows, HD:] = values[b * BLK : (b + 1) * BLK, a * HD : (a + 1) * HD]

        count = count + prompt.astype(jnp.int32)
    meta[COUNT] = count


def target(z, r):
    z = z[0]
    return jnp.where(r == 0, (3 - z) ^ 1, jnp.where(r == 1, z ^ 1, jnp.where(r == 2, 3 - z, z)))


def project_peer_kernel(z, c, here, grad, weight, seq, pos, depth, keys, values, out, meta, prompt, block, sems):
    r = pl.program_id(0)
    copies = [pltpu.make_async_copy(block, prompt.at[d], sems.at[d]) for d in range(DEVS)]

    @pl.when(r == 0)
    def _():
        make_layout(here, seq, pos, depth, keys, values, meta, block)
        for copy in copies:
            copy.start()

    out[0] = lax.dot_general(grad[...], weight[...], TN, preferred_element_type=jnp.float32).astype(jnp.bfloat16)

    @pl.when(r == 3)
    def _():
        for copy in copies:
            copy.wait()


def project_peer(z, c, here, out_grad, out_weight, slot_seq, slot_pos, fork_depth, keys, values):
    depth, rows = out_grad.shape
    cols = out_weight.shape[1] // 8
    block = (2, PCAP * BLK, 2 * HD)
    return pl.pallas_call(
        project_peer_kernel,
        out_shape=(
            jax.ShapeDtypeStruct((4, rows, cols), jnp.bfloat16),
            jax.ShapeDtypeStruct((META,), jnp.int32),
            jax.ShapeDtypeStruct((DEVS, *block), jnp.bfloat16),
        ),
        grid_spec=pltpu.PrefetchScalarGridSpec(
            num_scalar_prefetch=3,
            grid=(4,),
            in_specs=[
                pl.BlockSpec((depth, rows), lambda r, z, c, here: (0, 0)),
                pl.BlockSpec((depth, cols), lambda r, z, c, here: (0, target(z, r) * 2 + 1 - c[0])),
                *specs(SMEM, 3),
                pl.BlockSpec(keys.shape, lambda r, z, c, here: (0, 0)),
                pl.BlockSpec(values.shape, lambda r, z, c, here: (0, 0)),
            ],
            out_specs=(
                pl.BlockSpec((1, rows, cols), lambda r, z, c, here: (r, 0, 0)),
                pl.BlockSpec(memory_space=SMEM),
                pl.BlockSpec(memory_space=pl.ANY),
            ),
            scratch_shapes=[pltpu.VMEM(block, jnp.bfloat16), pltpu.SemaphoreType.DMA((DEVS,))],
        ),
        compiler_params=params(LIM),
        cost_estimate=pl.CostEstimate(flops=4 * 2 * rows * cols * depth, bytes_accessed=5 * 2**20, transcendentals=0),
        name="project_peer",
    )(z, c, here, out_grad, out_weight, slot_seq, slot_pos, fork_depth, keys, values)


def project_own_kernel(z, c, grad, weight, peer, send_a, keep_a, send_b, keep_b):
    r = pl.program_id(0)
    both = lax.dot_general(grad[...], weight[...], TN, preferred_element_type=jnp.float32)
    both = (both + peer[0].astype(jnp.float32)).astype(jnp.bfloat16)
    half = both.shape[1] // 2
    first, second = both[:, :half], both[:, half:]

    @pl.when(r < 2)
    def _():
        send_a[0] = first

    @pl.when(r >= 2)
    def _():
        keep_a[0] = first

    @pl.when(r % 2 == 0)
    def _():
        send_b[0] = second

    @pl.when(r % 2 == 1)
    def _():
        keep_b[0] = second


def project_own(z, c, out_grad, out_weight, peer):
    depth, rows = out_grad.shape
    cols = out_weight.shape[1] // 8
    part = jax.ShapeDtypeStruct((2, rows, cols // 2), jnp.bfloat16)

    def at(index):
        return pl.BlockSpec((1, rows, cols // 2), lambda r, z, c: (index(r), 0, 0))

    return pl.pallas_call(
        project_own_kernel,
        out_shape=(part, part, part, part),
        grid_spec=pltpu.PrefetchScalarGridSpec(
            num_scalar_prefetch=2,
            grid=(4,),
            in_specs=[
                pl.BlockSpec((depth, rows), lambda r, z, c: (0, 0)),
                pl.BlockSpec((depth, cols), lambda r, z, c: (0, target(z, r) * 2 + c[0])),
                pl.BlockSpec((1, rows, cols), lambda r, z, c: (r, 0, 0)),
            ],
            out_specs=(
                at(lambda r: jnp.where(r == 0, 1, 0)),
                at(lambda r: jnp.where(r == 3, 0, 1)),
                at(lambda r: jnp.where(r == 0, 1, 0)),
                at(lambda r: jnp.where(r >= 2, 0, 1)),
            ),
        ),
        compiler_params=params(LIM),
        cost_estimate=pl.CostEstimate(flops=4 * 2 * rows * cols * depth, bytes_accessed=7 * 2**20, transcendentals=0),
        name="project_own",
    )(z, c, out_grad, out_weight, peer)


def onward_kernel(keep, recv, own, out):
    for i, ref in enumerate((own, out)):
        ref[...] = (keep[i].astype(jnp.float32) + recv[i].astype(jnp.float32)).astype(jnp.bfloat16)


def onward(keep, recv):
    out = jax.ShapeDtypeStruct(keep.shape[1:], jnp.bfloat16)
    return pl.pallas_call(
        onward_kernel,
        out_shape=(out, out),
        in_specs=specs(VMEM, 2),
        out_specs=tuple(specs(VMEM, 2)),
        compiler_params=params(4),
        name="onward",
    )(keep, recv)


def attend_head(a, meta, q, k, v, gathered, parts, dq, dk, dv, ret, scratch):
    kc, vc, kt, qc, gc, gsum, dkc, dvc, ex, fx, dp = scratch
    gsum[...] = (parts[0][...].astype(jnp.float32) + parts[1][...].astype(jnp.float32)).astype(jnp.bfloat16)
    cols = slice(a * HD, (a + 1) * HD)
    for p in range(16):
        dev, src = place(meta[PLIST + p])
        kc[p * BLK : (p + 1) * BLK, :] = gathered[dev, src, :HD]
        vc[p * BLK : (p + 1) * BLK, :] = gathered[dev, src, HD:]

    lane = lax.broadcasted_iota(jnp.int32, (8, ROWS), 1)
    plim = jnp.zeros((8, ROWS), jnp.int32)
    llim = jnp.zeros((8, ROWS), jnp.int32)
    for j in range(BLK_DEV):
        src = rows_at(meta[ORDER + j])
        kc[PKEYS + j * BLK : PKEYS + (j + 1) * BLK, :] = k[src, cols]
        vc[PKEYS + j * BLK : PKEYS + (j + 1) * BLK, :] = v[src, cols]
        for h in range(2):
            to = slice(h * ROWS + j * BLK, h * ROWS + (j + 1) * BLK)
            qc[to, :] = q[src, (2 * a + h) * HD : (2 * a + h + 1) * HD]
            gc[to, :] = gsum[src, h * HD : (h + 1) * HD]
        here = (lane >= j * BLK) & (lane < (j + 1) * BLK)
        resp = meta[RESP + j]
        step = lane - (j * BLK - 1)
        plim = jnp.where(here, meta[BASE + j] + step * (1 - resp), plim)
        llim = jnp.where(here, (j * BLK + step) * resp, llim)
    kt[...] = kc[...].T
    sub = lax.broadcasted_iota(jnp.int32, (CHUNK, CHUNK), 0)

    for h in range(2):
        for half in range(ROWS // CHUNK):
            rows = slice(h * ROWS + half * CHUNK, h * ROWS + (half + 1) * CHUNK)
            qb = qc[rows, :]
            gb = gc[rows, :]
            lanes = slice(half * CHUNK, (half + 1) * CHUNK)
            pl_row = plim[:1, lanes]
            ll_row = llim[:1, lanes]
            chunks = PKEYS // CHUNK + half + 1
            total = jnp.zeros((1, CHUNK), jnp.float32)
            weighted = jnp.zeros((1, CHUNK), jnp.float32)
            for c in range(chunks):
                cut = slice(c * CHUNK, (c + 1) * CHUNK)
                raw = lax.dot_general(kc[cut, :], qb, NT, preferred_element_type=jnp.float32)
                dprob = lax.dot_general(vc[cut, :], gb, NT, preferred_element_type=jnp.float32)
                tanh_val = jnp.tanh(raw * (SCALE / SOFTCAP))
                if c * CHUNK < PKEYS:
                    seen = sub < pl_row - c * CHUNK
                else:
                    seen = sub < ll_row - (c * CHUNK - PKEYS)
                expo = jnp.where(seen, jnp.exp(SOFTCAP * tanh_val), 0.0)
                total = total + jnp.sum(expo, axis=0, keepdims=True)
                weighted = weighted + jnp.sum(expo * dprob, axis=0, keepdims=True)
                ex[cut, :] = expo
                fx[cut, :] = expo * (1.0 - tanh_val * tanh_val)
                dp[cut, :] = dprob
            inv = 1.0 / total
            delta = weighted * inv
            scaled = inv * SCALE
            dq_t = jnp.zeros((HD, CHUNK), jnp.float32)
            for c in range(chunks):
                cut = slice(c * CHUNK, (c + 1) * CHUNK)
                prob16 = (ex[cut, :] * inv).astype(jnp.bfloat16)
                dscore16 = (fx[cut, :] * ((dp[cut, :] - delta) * scaled)).astype(jnp.bfloat16)
                dv_part = jnp.dot(prob16, gb, preferred_element_type=jnp.float32)
                dk_part = jnp.dot(dscore16, qb, preferred_element_type=jnp.float32)
                dq_t = dq_t + jnp.dot(kt[:, cut], dscore16, preferred_element_type=jnp.float32)
                if h == 0 and (half == 0 or c == PKEYS // CHUNK + 1):
                    dvc[cut, :] = dv_part
                    dkc[cut, :] = dk_part
                else:
                    dvc[cut, :] += dv_part
                    dkc[cut, :] += dk_part
            dq_rows = dq_t.T.astype(jnp.bfloat16)
            for j in range(CHUNK // BLK):
                dst = rows_at(meta[ORDER + half * (CHUNK // BLK) + j])
                dq[dst, h * HD : (h + 1) * HD] = dq_rows[j * BLK : (j + 1) * BLK, :]

    ret[...] = jnp.zeros(ret.shape, ret.dtype)
    for p in range(16):
        dev, dst = place(meta[PLIST + p])
        src = slice(p * BLK, (p + 1) * BLK)
        ret[dev, dst, :HD] = dkc[src, :].astype(jnp.bfloat16)
        ret[dev, dst, HD:] = dvc[src, :].astype(jnp.bfloat16)
    for j in range(BLK_DEV):
        dst = rows_at(meta[ORDER + j])
        src = slice(PKEYS + j * BLK, PKEYS + (j + 1) * BLK)
        dk[dst, cols] = dkc[src, :].astype(jnp.bfloat16)
        dv[dst, cols] = dvc[src, :].astype(jnp.bfloat16)


def attend_kernel(
    meta, q, k, v, gathered, own_a, last_a, own_b, last_b,
    dq, dk, dv, ret,
    qs, ks, vs, gs, ps, dqs, dks, dvs, rets, sem_in, sem_out, *scratch,
):
    loads = [
        (own_a, ps.at[0, 0]), (last_a, ps.at[0, 1]), (gathered.at[:, 0], gs.at[0]), (k, ks), (v, vs), (q, qs),
        (own_b, ps.at[1, 0]), (last_b, ps.at[1, 1]), (gathered.at[:, 1], gs.at[1]),
    ]
    loads = [pltpu.make_async_copy(src, dst, sem_in.at[i]) for i, (src, dst) in enumerate(loads)]
    for copy in loads:
        copy.start()
    stores = [
        (rets.at[0], ret.at[:, 0]), (dqs.at[0], dq.at[:, pl.ds(0, 2 * HD)]),
        (rets.at[1], ret.at[:, 1]), (dqs.at[1], dq.at[:, pl.ds(2 * HD, 2 * HD)]), (dks, dk), (dvs, dv),
    ]
    stores = [pltpu.make_async_copy(src, dst, sem_out.at[i]) for i, (src, dst) in enumerate(stores)]
    for a in range(2):
        for copy in loads[6 * a : 6 + 3 * a]:
            copy.wait()
        parts = [ps.at[a, i] for i in range(2)]
        attend_head(a, meta, qs, ks, vs, gs.at[a], parts, dqs.at[a], dks, dvs, rets.at[a], scratch)
        for copy in stores[2 * a : 2 + 4 * a]:
            copy.start()
    for copy in stores:
        copy.wait()


def attend(meta, queries, keys, values, gathered, parts):
    return pl.pallas_call(
        attend_kernel,
        out_shape=(
            jax.ShapeDtypeStruct(queries.shape, jnp.bfloat16),
            jax.ShapeDtypeStruct(keys.shape, jnp.bfloat16),
            jax.ShapeDtypeStruct(values.shape, jnp.bfloat16),
            jax.ShapeDtypeStruct(gathered.shape, jnp.bfloat16),
        ),
        in_specs=specs(SMEM, 1) + specs(pl.ANY, 8),
        out_specs=tuple(specs(pl.ANY, 4)),
        scratch_shapes=[
            pltpu.VMEM(queries.shape, jnp.bfloat16),
            pltpu.VMEM(keys.shape, jnp.bfloat16),
            pltpu.VMEM(values.shape, jnp.bfloat16),
            pltpu.VMEM((2, DEVS, PCAP * BLK, 2 * HD), jnp.bfloat16),
            pltpu.VMEM((2, 2, ROWS, 2 * HD), jnp.bfloat16),
            pltpu.VMEM((2, ROWS, 2 * HD), jnp.bfloat16),
            pltpu.VMEM(keys.shape, jnp.bfloat16),
            pltpu.VMEM(values.shape, jnp.bfloat16),
            pltpu.VMEM((2, DEVS, PCAP * BLK, 2 * HD), jnp.bfloat16),
            pltpu.SemaphoreType.DMA((9,)),
            pltpu.SemaphoreType.DMA((6,)),
            pltpu.VMEM((KEYS, HD), jnp.bfloat16),
            pltpu.VMEM((KEYS, HD), jnp.bfloat16),
            pltpu.VMEM((HD, KEYS), jnp.bfloat16),
            pltpu.VMEM((2 * ROWS, HD), jnp.bfloat16),
            pltpu.VMEM((2 * ROWS, HD), jnp.bfloat16),
            pltpu.VMEM((ROWS, 2 * HD), jnp.bfloat16),
            pltpu.VMEM((KEYS, HD), jnp.float32),
            pltpu.VMEM((KEYS, HD), jnp.float32),
            pltpu.VMEM((KEYS, CHUNK), jnp.float32),
            pltpu.VMEM((KEYS, CHUNK), jnp.float32),
            pltpu.VMEM((KEYS, CHUNK), jnp.float32),
        ],
        compiler_params=params(LIM),
        cost_estimate=pl.CostEstimate(flops=4 * 10**9, bytes_accessed=8 * 2**20, transcendentals=6 * 10**6),
        name="attend",
    )(meta, queries, keys, values, gathered, *parts)


def finish_kernel(meta, own_k, own_v, ret, dk, dv):
    for i, (own, out) in enumerate(((own_k, dk), (own_v, dv))):
        out[...] = own[...]
        for r in range(PCAP):

            @pl.when(meta[COUNT] > r)
            def _(r=r, i=i, out=out):
                rows = slice(r * BLK, (r + 1) * BLK)
                for a in range(2):
                    total = ret[0, a, rows, i * HD : (i + 1) * HD].astype(jnp.float32)
                    for d in range(1, DEVS):
                        total = total + ret[d, a, rows, i * HD : (i + 1) * HD].astype(jnp.float32)
                    at = rows_at(meta[ORDER + BLK_DEV - 1 - r])
                    out[at, a * HD : (a + 1) * HD] = total.astype(jnp.bfloat16)


def finish(meta, own_k, own_v, ret):
    out = jax.ShapeDtypeStruct(own_k.shape, jnp.bfloat16)
    return pl.pallas_call(
        finish_kernel,
        out_shape=(out, out),
        in_specs=specs(SMEM, 1) + specs(VMEM, 3),
        out_specs=tuple(specs(VMEM, 2)),
        compiler_params=params(8),
        name="finish",
    )(meta, own_k, own_v, ret)


def scalar(axis):
    return lax.axis_index(axis).astype(jnp.int32).reshape(1)


def shards(out_grad, out_weight, query_states, key_states, value_states, slot_seq, slot_pos, fork_depth):
    here, z, c = scalar("seq"), scalar("mp"), scalar("section")
    pair_a = [(i, i ^ 1) for i in range(4)]
    pair_b = [(i, 3 - i) for i in range(4)]
    out_grad, out_weight = out_grad.T, out_weight.T

    slots = (slot_seq, slot_pos, fork_depth)
    peer, meta, prompt = project_peer(z, c, here, out_grad, out_weight, *slots, key_states, value_states)
    peer = lax.ppermute(peer, "section", [(0, 1), (1, 0)])
    gathered = lax.all_to_all(prompt, "seq", 0, 0, tiled=True)
    send_a, keep_a, send_b, keep_b = project_own(z, c, out_grad, out_weight, peer)
    recv_a = lax.ppermute(send_a, "mp", pair_a)
    recv_b = lax.ppermute(send_b, "mp", pair_b)
    own_a, next_a = onward(keep_a, recv_a)
    last_a = lax.ppermute(next_a, "mp", pair_b)
    own_b, next_b = onward(keep_b, recv_b)
    last_b = lax.ppermute(next_b, "mp", pair_a)
    parts = (own_a, last_a, own_b, last_b)
    dq, own_k, own_v, ret = attend(meta, query_states, key_states, value_states, gathered, parts)
    ret = lax.all_to_all(ret, "seq", 0, 0, tiled=True)
    dk, dv = finish(meta, own_k, own_v, ret)
    return dq, dk, dv


def solution(mesh):
    wide = P("seq", ("mp", "section"))
    return jax.shard_map(
        shards,
        mesh=mesh,
        in_specs=(wide, P(None, ("mp", "section")), wide, wide, wide, P(), P(), P()),
        out_specs=(wide, wide, wide),
        check_vma=False,
    )
```

```python
import jax
import jax.numpy as jnp
from jax import lax
from jax.experimental import pallas as pl
from jax.experimental.pallas import tpu as pltpu
from jax.sharding import PartitionSpec as P

HD = 128
BLK = 64
BLK_DEV = 8
PCAP = 2
DEVS = 16
ROWS = BLK * BLK_DEV
PKEYS = 16 * BLK
KEYS = PKEYS + ROWS
CHUNK = 256

SCALE = 144.0 ** (-0.5)
SOFTCAP = 50.0
LOG2E = 1.4426950408889634

PLIST = 0
ORDER = 16
BASE = 24
RESP = 32
COUNT = 40
SPARE = 41
META = 48

LIM = 60
OWNLIM = 60

SMEM = pltpu.MemorySpace.SMEM
VMEM = pltpu.MemorySpace.VMEM
HBM = pltpu.MemorySpace.HBM
NT = (((1,), (1,)), ((), ()))
TN = (((0,), (0,)), ((), ()))


def params(mib):
    return pltpu.CompilerParams(vmem_limit_bytes=mib * 2**20)


def specs(space, n):
    return [pl.BlockSpec(memory_space=space)] * n


def rows_at(i):
    return pl.ds(pl.multiple_of(i * BLK, BLK), BLK)


def place(slot):
    return lax.shift_right_logical(slot, 1), rows_at(slot & 1)


def make_layout(here, seq, pos, depth, keys, values, meta, block):
    me = here[0]

    for dev in range(DEVS):
        count = jnp.int32(0)
        for b in range(BLK_DEV):
            slot = dev * BLK_DEV + b
            prompt = seq[slot] == 0
            at = jnp.where(prompt, PLIST + pos[slot], SPARE)
            meta[at] = dev * PCAP + jnp.minimum(count, PCAP - 1)
            count = count + prompt.astype(jnp.int32)

    count = jnp.int32(0)
    block[...] = jnp.zeros(block.shape, block.dtype)
    for b in range(BLK_DEV):
        slot = me * BLK_DEV + b
        prompt = seq[slot] == 0
        at = jnp.where(prompt, BLK_DEV - 1 - count, pos[slot])
        meta[ORDER + at] = jnp.int32(b)
        meta[RESP + at] = 1 - prompt.astype(jnp.int32)
        meta[BASE + at] = jnp.where(prompt, pos[slot], depth[jnp.maximum(seq[slot] - 1, 0)]) * BLK

        @pl.when(prompt)
        def _(count=count, b=b):
            rows = rows_at(jnp.minimum(count, PCAP - 1))
            for a in range(2):
                block[a, rows, :HD] = keys[b * BLK : (b + 1) * BLK, a * HD : (a + 1) * HD]
                block[a, rows, HD:] = values[b * BLK : (b + 1) * BLK, a * HD : (a + 1) * HD]

        count = count + prompt.astype(jnp.int32)
    meta[COUNT] = count


def target(z, r):
    z = z[0]
    return jnp.where(r == 0, (3 - z) ^ 1, jnp.where(r == 1, z ^ 1, jnp.where(r == 2, 3 - z, z)))


def project_peer_kernel(z, c, here, grad, weight, seq, pos, depth, keys, values, out, meta, prompt, block, sems):
    r = pl.program_id(0)
    copies = [pltpu.make_async_copy(block, prompt.at[d], sems.at[d]) for d in range(DEVS)]

    def product():
        out[0] = lax.dot_general(grad[...], weight[...], TN, preferred_element_type=jnp.float32).astype(jnp.bfloat16)

    @pl.when(r == 0)
    def _():
        make_layout(here, seq, pos, depth, keys, values, meta, block)
        for copy in copies:
            copy.start()
        product()

    @pl.when(r > 0)
    def _():
        product()

    @pl.when(r == 3)
    def _():
        for copy in copies:
            copy.wait()


def project_peer(z, c, here, out_grad, out_weight, slot_seq, slot_pos, fork_depth, keys, values):
    depth, rows = out_grad.shape
    cols = out_weight.shape[1] // 8
    block = (2, PCAP * BLK, 2 * HD)
    return pl.pallas_call(
        project_peer_kernel,
        out_shape=(
            jax.ShapeDtypeStruct((4, rows, cols), jnp.bfloat16),
            jax.ShapeDtypeStruct((META,), jnp.int32),
            jax.ShapeDtypeStruct((DEVS, *block), jnp.bfloat16),
        ),
        grid_spec=pltpu.PrefetchScalarGridSpec(
            num_scalar_prefetch=3,
            grid=(4,),
            in_specs=[
                pl.BlockSpec((depth, rows), lambda r, z, c, here: (0, 0)),
                pl.BlockSpec((depth, cols), lambda r, z, c, here: (0, target(z, r) * 2 + 1 - c[0])),
                *specs(SMEM, 3),
                pl.BlockSpec(keys.shape, lambda r, z, c, here: (0, 0)),
                pl.BlockSpec(values.shape, lambda r, z, c, here: (0, 0)),
            ],
            out_specs=(
                pl.BlockSpec((1, rows, cols), lambda r, z, c, here: (r, 0, 0)),
                pl.BlockSpec(memory_space=SMEM),
                pl.BlockSpec(memory_space=pl.ANY),
            ),
            scratch_shapes=[pltpu.VMEM(block, jnp.bfloat16), pltpu.SemaphoreType.DMA((DEVS,))],
        ),
        compiler_params=params(LIM),
        cost_estimate=pl.CostEstimate(flops=4 * 2 * rows * cols * depth, bytes_accessed=5 * 2**20, transcendentals=0),
        name="project_peer",
    )(z, c, here, out_grad, out_weight, slot_seq, slot_pos, fork_depth, keys, values)


def project_own_kernel(z, c, grad, weight, peer, send_a, keep_a, send_b, keep_b):
    r = pl.program_id(0)
    both = lax.dot_general(grad[...], weight[...], TN, preferred_element_type=jnp.float32)
    both = (both + peer[0].astype(jnp.float32)).astype(jnp.bfloat16)
    half = both.shape[1] // 2
    first, second = both[:, :half], both[:, half:]

    @pl.when(r < 2)
    def _():
        send_a[0] = first

    @pl.when(r >= 2)
    def _():
        keep_a[0] = first

    @pl.when(r % 2 == 0)
    def _():
        send_b[0] = second

    @pl.when(r % 2 == 1)
    def _():
        keep_b[0] = second


def project_own(z, c, out_grad, out_weight, peer):
    depth, rows = out_grad.shape
    cols = out_weight.shape[1] // 8
    part = jax.ShapeDtypeStruct((2, rows, cols // 2), jnp.bfloat16)

    def at(index):
        return pl.BlockSpec((1, rows, cols // 2), lambda r, z, c: (index(r), 0, 0))

    return pl.pallas_call(
        project_own_kernel,
        out_shape=(part, part, part, part),
        grid_spec=pltpu.PrefetchScalarGridSpec(
            num_scalar_prefetch=2,
            grid=(4,),
            in_specs=[
                pl.BlockSpec((depth, rows), lambda r, z, c: (0, 0)),
                pl.BlockSpec((depth, cols), lambda r, z, c: (0, target(z, r) * 2 + c[0])),
                pl.BlockSpec((1, rows, cols), lambda r, z, c: (r, 0, 0)),
            ],
            out_specs=(
                at(lambda r: jnp.where(r == 0, 1, 0)),
                at(lambda r: jnp.where(r == 3, 0, 1)),
                at(lambda r: jnp.where(r == 0, 1, 0)),
                at(lambda r: jnp.where(r >= 2, 0, 1)),
            ),
        ),
        compiler_params=params(OWNLIM),
        cost_estimate=pl.CostEstimate(flops=4 * 2 * rows * cols * depth, bytes_accessed=7 * 2**20, transcendentals=0),
        name="project_own",
    )(z, c, out_grad, out_weight, peer)


def visible(meta, seen):
    lane = lax.broadcasted_iota(jnp.int32, (8, ROWS), 1)
    prompt = jnp.zeros((8, ROWS), jnp.int32)
    own = jnp.zeros((8, ROWS), jnp.int32)
    for j in range(BLK_DEV):
        here = (lane >= j * BLK) & (lane < (j + 1) * BLK)
        resp = meta[RESP + j]
        step = lane - (j * BLK - 1)
        prompt = jnp.where(here, meta[BASE + j] + step * (1 - resp), prompt)
        own = jnp.where(here, (j * BLK + step) * resp, own)
    row = lax.broadcasted_iota(jnp.int32, (8, ROWS), 0)
    for start, limit, size in ((0, prompt - row, PKEYS), (PKEYS, own - row, ROWS)):
        for r in range(0, size, 8):
            seen[start + r : start + r + 8, :] = jnp.where(limit > r, 1.0, 0.0)


def attend_head(a, meta, q, k, v, gathered, parts, dq, dk, dv, ret, scratch):
    kc, vc, kt, qc, gc, gsum, dkc, dvc, ex, fx, dp, seen = scratch
    gsum[...] = (parts[0][...].astype(jnp.float32) + parts[1][...].astype(jnp.float32)).astype(jnp.bfloat16)
    cols = slice(a * HD, (a + 1) * HD)
    for p in range(16):
        dev, src = place(meta[PLIST + p])
        kc[p * BLK : (p + 1) * BLK, :] = gathered[dev, src, :HD]
        vc[p * BLK : (p + 1) * BLK, :] = gathered[dev, src, HD:]

    for j in range(BLK_DEV):
        src = rows_at(meta[ORDER + j])
        kc[PKEYS + j * BLK : PKEYS + (j + 1) * BLK, :] = k[src, cols]
        vc[PKEYS + j * BLK : PKEYS + (j + 1) * BLK, :] = v[src, cols]
        for h in range(2):
            to = slice(h * ROWS + j * BLK, h * ROWS + (j + 1) * BLK)
            qc[to, :] = q[src, (2 * a + h) * HD : (2 * a + h + 1) * HD]
            gc[to, :] = gsum[src, h * HD : (h + 1) * HD]
    kt[...] = kc[...].T

    blocks = [(h, half) for h in range(2) for half in range(ROWS // CHUNK)]
    count = [PKEYS // CHUNK + half + 1 for h, half in blocks]
    sums = {}

    def scores(n, c):
        h, half = blocks[n]
        rows = slice(h * ROWS + half * CHUNK, h * ROWS + (half + 1) * CHUNK)
        cut = slice(c * CHUNK, (c + 1) * CHUNK)
        raw = lax.dot_general(kc[cut, :], qc[rows, :], NT, preferred_element_type=jnp.float32)
        dprob = lax.dot_general(vc[cut, :], gc[rows, :], NT, preferred_element_type=jnp.float32)
        tanh_val = jnp.tanh(raw * (SCALE / SOFTCAP))
        expo = jnp.exp2(tanh_val * (SOFTCAP * LOG2E)) * seen[cut, half * CHUNK : (half + 1) * CHUNK]
        total, weighted = sums.get(n, (0.0, 0.0))
        total = total + jnp.sum(expo, axis=0, keepdims=True)
        weighted = weighted + jnp.sum(expo * dprob, axis=0, keepdims=True)
        sums[n] = (total, weighted)
        ex[n % 2, cut, :] = expo
        fx[n % 2, cut, :] = expo * (1.0 - tanh_val * tanh_val)
        dp[n % 2, cut, :] = dprob

    def gradients(n, c, dq_t):
        h, half = blocks[n]
        rows = slice(h * ROWS + half * CHUNK, h * ROWS + (half + 1) * CHUNK)
        cut = slice(c * CHUNK, (c + 1) * CHUNK)
        inv, delta, scaled = sums[n]
        prob16 = (ex[n % 2, cut, :] * inv).astype(jnp.bfloat16)
        dscore16 = (fx[n % 2, cut, :] * ((dp[n % 2, cut, :] - delta) * scaled)).astype(jnp.bfloat16)
        dv_part = jnp.dot(prob16, gc[rows, :], preferred_element_type=jnp.float32)
        dk_part = jnp.dot(dscore16, qc[rows, :], preferred_element_type=jnp.float32)
        if h == 0 and (half == 0 or c == PKEYS // CHUNK + 1):
            dvc[cut, :] = dv_part
            dkc[cut, :] = dk_part
        else:
            dvc[cut, :] += dv_part
            dkc[cut, :] += dk_part
        return dq_t + jnp.dot(kt[:, cut], dscore16, preferred_element_type=jnp.float32)

    for n in range(len(blocks) + 1):
        if n:
            total, weighted = sums[n - 1]
            inv = 1.0 / total
            sums[n - 1] = (inv, weighted * inv, inv * SCALE)
            dq_t = jnp.zeros((HD, CHUNK), jnp.float32)
        for c in range(KEYS // CHUNK):
            if n < len(blocks) and c < count[n]:
                scores(n, c)
            if n and c < count[n - 1]:
                dq_t = gradients(n - 1, c, dq_t)
        if n:
            h, half = blocks[n - 1]
            dq_rows = dq_t.T.astype(jnp.bfloat16)
            for j in range(CHUNK // BLK):
                dst = rows_at(meta[ORDER + half * (CHUNK // BLK) + j])
                dq[dst, h * HD : (h + 1) * HD] = dq_rows[j * BLK : (j + 1) * BLK, :]

    ret[...] = jnp.zeros(ret.shape, ret.dtype)
    for p in range(16):
        dev, dst = place(meta[PLIST + p])
        src = slice(p * BLK, (p + 1) * BLK)
        ret[dev, dst, :HD] = dkc[src, :].astype(jnp.bfloat16)
        ret[dev, dst, HD:] = dvc[src, :].astype(jnp.bfloat16)
    for j in range(BLK_DEV):
        dst = rows_at(meta[ORDER + j])
        src = slice(PKEYS + j * BLK, PKEYS + (j + 1) * BLK)
        dk[dst, cols] = dkc[src, :].astype(jnp.bfloat16)
        dv[dst, cols] = dvc[src, :].astype(jnp.bfloat16)


def attend_kernel(
    meta, q, k, v, gathered, own_a, last_a, own_b, last_b,
    dq, dk, dv, ret,
    qs, ks, vs, dqs, dks, dvs, rets, sem_in, sem_out, *scratch,
):
    loads = [(k, ks), (v, vs), (q, qs)]
    loads = [pltpu.make_async_copy(src, dst, sem_in.at[i]) for i, (src, dst) in enumerate(loads)]
    for copy in loads:
        copy.start()
    stores = [
        (rets.at[0], ret.at[:, 0]), (dqs.at[0], dq.at[:, pl.ds(0, 2 * HD)]),
        (rets.at[1], ret.at[:, 1]), (dqs.at[1], dq.at[:, pl.ds(2 * HD, 2 * HD)]), (dks, dk), (dvs, dv),
    ]
    stores = [pltpu.make_async_copy(src, dst, sem_out.at[i]) for i, (src, dst) in enumerate(stores)]
    visible(meta, scratch[-1])
    for copy in loads:
        copy.wait()
    for a in range(2):
        parts = (own_b, last_b) if a else (own_a, last_a)
        attend_head(a, meta, qs, ks, vs, gathered.at[:, a], parts, dqs.at[a], dks, dvs, rets.at[a], scratch)
        for copy in stores[2 * a : 2 + 4 * a]:
            copy.start()
    for copy in stores:
        copy.wait()


def attend(meta, queries, keys, values, gathered, parts):
    return pl.pallas_call(
        attend_kernel,
        out_shape=(
            jax.ShapeDtypeStruct(queries.shape, jnp.bfloat16),
            jax.ShapeDtypeStruct(keys.shape, jnp.bfloat16),
            jax.ShapeDtypeStruct(values.shape, jnp.bfloat16),
            jax.ShapeDtypeStruct(gathered.shape, jnp.bfloat16),
        ),
        in_specs=specs(SMEM, 1) + specs(HBM, 3) + specs(VMEM, 5),
        out_specs=tuple(specs(pl.ANY, 4)),
        scratch_shapes=[
            pltpu.VMEM(queries.shape, jnp.bfloat16),
            pltpu.VMEM(keys.shape, jnp.bfloat16),
            pltpu.VMEM(values.shape, jnp.bfloat16),
            pltpu.VMEM((2, ROWS, 2 * HD), jnp.bfloat16),
            pltpu.VMEM(keys.shape, jnp.bfloat16),
            pltpu.VMEM(values.shape, jnp.bfloat16),
            pltpu.VMEM((2, DEVS, PCAP * BLK, 2 * HD), jnp.bfloat16),
            pltpu.SemaphoreType.DMA((3,)),
            pltpu.SemaphoreType.DMA((6,)),
            pltpu.VMEM((KEYS, HD), jnp.bfloat16),
            pltpu.VMEM((KEYS, HD), jnp.bfloat16),
            pltpu.VMEM((HD, KEYS), jnp.bfloat16),
            pltpu.VMEM((2 * ROWS, HD), jnp.bfloat16),
            pltpu.VMEM((2 * ROWS, HD), jnp.bfloat16),
            pltpu.VMEM((ROWS, 2 * HD), jnp.bfloat16),
            pltpu.VMEM((KEYS, HD), jnp.float32),
            pltpu.VMEM((KEYS, HD), jnp.float32),
            pltpu.VMEM((2, KEYS, CHUNK), jnp.float32),
            pltpu.VMEM((2, KEYS, CHUNK), jnp.float32),
            pltpu.VMEM((2, KEYS, CHUNK), jnp.float32),
            pltpu.VMEM((KEYS, ROWS), jnp.float32),
        ],
        compiler_params=params(32),
        cost_estimate=pl.CostEstimate(flops=4 * 10**9, bytes_accessed=8 * 2**20, transcendentals=6 * 10**6),
        name="attend",
    )(meta, queries, keys, values, gathered, *parts)


def finish_kernel(meta, own_k, own_v, ret, dk, dv):
    for i, (own, out) in enumerate(((own_k, dk), (own_v, dv))):
        out[...] = own[...]
        for r in range(PCAP):

            @pl.when(meta[COUNT] > r)
            def _(r=r, i=i, out=out):
                rows = slice(r * BLK, (r + 1) * BLK)
                for a in range(2):
                    total = ret[0, a, rows, i * HD : (i + 1) * HD].astype(jnp.float32)
                    for d in range(1, DEVS):
                        total = total + ret[d, a, rows, i * HD : (i + 1) * HD].astype(jnp.float32)
                    at = rows_at(meta[ORDER + BLK_DEV - 1 - r])
                    out[at, a * HD : (a + 1) * HD] = total.astype(jnp.bfloat16)


def finish(meta, own_k, own_v, ret):
    out = jax.ShapeDtypeStruct(own_k.shape, jnp.bfloat16)
    return pl.pallas_call(
        finish_kernel,
        out_shape=(out, out),
        in_specs=specs(SMEM, 1) + specs(VMEM, 3),
        out_specs=tuple(specs(VMEM, 2)),
        compiler_params=params(8),
        name="finish",
    )(meta, own_k, own_v, ret)


def scalar(axis):
    return lax.axis_index(axis).astype(jnp.int32).reshape(1)


def shards(out_grad, out_weight, query_states, key_states, value_states, slot_seq, slot_pos, fork_depth):
    here, z, c = scalar("seq"), scalar("mp"), scalar("section")
    pair_a = [(i, i ^ 1) for i in range(4)]
    pair_b = [(i, 3 - i) for i in range(4)]
    out_grad, out_weight = out_grad.T, out_weight.T

    slots = (slot_seq, slot_pos, fork_depth)
    peer, meta, prompt = project_peer(z, c, here, out_grad, out_weight, *slots, key_states, value_states)
    peer = lax.ppermute(peer, "section", [(0, 1), (1, 0)])
    gathered = lax.all_to_all(prompt, "seq", 0, 0, tiled=True)
    send_a, keep_a, send_b, keep_b = project_own(z, c, out_grad, out_weight, peer)
    recv_a = lax.ppermute(send_a, "mp", pair_a)
    recv_b = lax.ppermute(send_b, "mp", pair_b)
    next_a = (keep_a[1].astype(jnp.float32) + recv_a[1].astype(jnp.float32)).astype(jnp.bfloat16)
    next_b = (keep_b[1].astype(jnp.float32) + recv_b[1].astype(jnp.float32)).astype(jnp.bfloat16)
    keep_a, recv_a, keep_b, recv_b, next_a, next_b = lax.optimization_barrier(
        (keep_a, recv_a, keep_b, recv_b, next_a, next_b)
    )
    own_a = (keep_a[0].astype(jnp.float32) + recv_a[0].astype(jnp.float32)).astype(jnp.bfloat16)
    own_b = (keep_b[0].astype(jnp.float32) + recv_b[0].astype(jnp.float32)).astype(jnp.bfloat16)
    last_a = lax.ppermute(next_a, "mp", pair_b)
    last_b = lax.ppermute(next_b, "mp", pair_a)
    parts = (own_a, last_a, own_b, last_b)
    dq, own_k, own_v, ret = attend(meta, query_states, key_states, value_states, gathered, parts)
    ret = lax.all_to_all(ret, "seq", 0, 0, tiled=True)
    dk, dv = finish(meta, own_k, own_v, ret)
    return dq, dk, dv


def solution(mesh):
    wide = P("seq", ("mp", "section"))
    return jax.shard_map(
        shards,
        mesh=mesh,
        in_specs=(wide, P(None, ("mp", "section")), wide, wide, wide, P(), P(), P()),
        out_specs=(wide, wide, wide),
        check_vma=False,
    )
```

```python
import jax
import jax.numpy as jnp
from jax import lax
from jax.experimental import pallas as pl
from jax.experimental.pallas import tpu as pltpu
from jax.sharding import PartitionSpec as P

HD = 128
BLK = 64
BLK_DEV = 8
PCAP = 2
DEVS = 16
ROWS = BLK * BLK_DEV
PKEYS = 16 * BLK
KEYS = PKEYS + ROWS
CHUNK = 256

SCALE = 144.0 ** (-0.5)
SOFTCAP = 50.0
LOG2E = 1.4426950408889634

PLIST = 0
ORDER = 16
BASE = 24
RESP = 32
COUNT = 40
SPARE = 41
META = 48

LIM = 60
OWNLIM = 60

SMEM = pltpu.MemorySpace.SMEM
VMEM = pltpu.MemorySpace.VMEM
HBM = pltpu.MemorySpace.HBM
NT = (((1,), (1,)), ((), ()))
TN = (((0,), (0,)), ((), ()))


def params(mib):
    return pltpu.CompilerParams(vmem_limit_bytes=mib * 2**20)


def specs(space, n):
    return [pl.BlockSpec(memory_space=space)] * n


def rows_at(i):
    return pl.ds(pl.multiple_of(i * BLK, BLK), BLK)


def place(slot):
    return lax.shift_right_logical(slot, 1), rows_at(slot & 1)


BACK = tuple(range(DEVS - 1, -1, -1))


def make_layout(here, seq, pos, depth, keys, values, meta, block):
    me = here[0]

    for dev in range(DEVS):
        count = jnp.int32(0)
        for b in range(BLK_DEV):
            slot = dev * BLK_DEV + b
            prompt = seq[slot] == 0
            at = jnp.where(prompt, PLIST + pos[slot], SPARE)
            meta[at] = dev * PCAP + jnp.minimum(count, PCAP - 1)
            count = count + prompt.astype(jnp.int32)

    count = jnp.int32(0)
    block[...] = jnp.zeros(block.shape, block.dtype)
    for b in range(BLK_DEV):
        slot = me * BLK_DEV + b
        prompt = seq[slot] == 0
        at = jnp.where(prompt, BLK_DEV - 1 - count, pos[slot])
        meta[ORDER + at] = jnp.int32(b)
        meta[RESP + at] = 1 - prompt.astype(jnp.int32)
        meta[BASE + at] = jnp.where(prompt, pos[slot], depth[jnp.maximum(seq[slot] - 1, 0)]) * BLK

        @pl.when(prompt)
        def _(count=count, b=b):
            rows = rows_at(jnp.minimum(count, PCAP - 1))
            for a in range(2):
                block[a, rows, :HD] = keys[b * BLK : (b + 1) * BLK, a * HD : (a + 1) * HD]
                block[a, rows, HD:] = values[b * BLK : (b + 1) * BLK, a * HD : (a + 1) * HD]

        count = count + prompt.astype(jnp.int32)
    meta[COUNT] = count


def target(z, r):
    z = z[0]
    return jnp.where(r == 0, (3 - z) ^ 1, jnp.where(r == 1, z ^ 1, jnp.where(r == 2, 3 - z, z)))


def project_peer_kernel(z, c, here, grad, weight, seq, pos, depth, keys, values, out, meta, prompt, block, sems):
    r = pl.program_id(0)
    copies = [pltpu.make_async_copy(block, prompt.at[d], sems.at[d]) for d in range(DEVS)]

    def product():
        out[0] = lax.dot_general(grad[...], weight[...], TN, preferred_element_type=jnp.float32).astype(jnp.bfloat16)

    @pl.when(r == 0)
    def _():
        make_layout(here, seq, pos, depth, keys, values, meta, block)
        for copy in copies:
            copy.start()
        product()

    @pl.when(r > 0)
    def _():
        product()

    @pl.when(r == 3)
    def _():
        for copy in copies:
            copy.wait()


def project_peer(z, c, here, out_grad, out_weight, slot_seq, slot_pos, fork_depth, keys, values):
    depth, rows = out_grad.shape
    cols = out_weight.shape[1] // 8
    block = (2, PCAP * BLK, 2 * HD)
    return pl.pallas_call(
        project_peer_kernel,
        out_shape=(
            jax.ShapeDtypeStruct((4, rows, cols), jnp.bfloat16),
            jax.ShapeDtypeStruct((META,), jnp.int32),
            jax.ShapeDtypeStruct((DEVS, *block), jnp.bfloat16),
        ),
        grid_spec=pltpu.PrefetchScalarGridSpec(
            num_scalar_prefetch=3,
            grid=(4,),
            in_specs=[
                pl.BlockSpec((depth, rows), lambda r, z, c, here: (0, 0)),
                pl.BlockSpec((depth, cols), lambda r, z, c, here: (0, target(z, r) * 2 + 1 - c[0])),
                *specs(SMEM, 3),
                pl.BlockSpec(keys.shape, lambda r, z, c, here: (0, 0)),
                pl.BlockSpec(values.shape, lambda r, z, c, here: (0, 0)),
            ],
            out_specs=(
                pl.BlockSpec((1, rows, cols), lambda r, z, c, here: (r, 0, 0)),
                pl.BlockSpec(memory_space=SMEM),
                pl.BlockSpec(memory_space=pl.ANY),
            ),
            scratch_shapes=[pltpu.VMEM(block, jnp.bfloat16), pltpu.SemaphoreType.DMA((DEVS,))],
        ),
        compiler_params=params(LIM),
        cost_estimate=pl.CostEstimate(flops=4 * 2 * rows * cols * depth, bytes_accessed=5 * 2**20, transcendentals=0),
        name="project_peer",
    )(z, c, here, out_grad, out_weight, slot_seq, slot_pos, fork_depth, keys, values)


def project_own_kernel(z, c, grad, weight, peer, send_a, keep_a, send_b, keep_b):
    r = pl.program_id(0)
    both = lax.dot_general(grad[...], weight[...], TN, preferred_element_type=jnp.float32)
    both = (both + peer[0].astype(jnp.float32)).astype(jnp.bfloat16)
    half = both.shape[1] // 2
    first, second = both[:, :half], both[:, half:]

    @pl.when(r < 2)
    def _():
        send_a[0] = first

    @pl.when(r >= 2)
    def _():
        keep_a[0] = first

    @pl.when(r % 2 == 0)
    def _():
        send_b[0] = second

    @pl.when(r % 2 == 1)
    def _():
        keep_b[0] = second


def project_own(z, c, out_grad, out_weight, peer):
    depth, rows = out_grad.shape
    cols = out_weight.shape[1] // 8
    part = jax.ShapeDtypeStruct((2, rows, cols // 2), jnp.bfloat16)

    def at(index):
        return pl.BlockSpec((1, rows, cols // 2), lambda r, z, c: (index(r), 0, 0))

    return pl.pallas_call(
        project_own_kernel,
        out_shape=(part, part, part, part),
        grid_spec=pltpu.PrefetchScalarGridSpec(
            num_scalar_prefetch=2,
            grid=(4,),
            in_specs=[
                pl.BlockSpec((depth, rows), lambda r, z, c: (0, 0)),
                pl.BlockSpec((depth, cols), lambda r, z, c: (0, target(z, r) * 2 + c[0])),
                pl.BlockSpec((1, rows, cols), lambda r, z, c: (r, 0, 0)),
            ],
            out_specs=(
                at(lambda r: jnp.where(r == 0, 1, 0)),
                at(lambda r: jnp.where(r == 3, 0, 1)),
                at(lambda r: jnp.where(r == 0, 1, 0)),
                at(lambda r: jnp.where(r >= 2, 0, 1)),
            ),
        ),
        compiler_params=params(OWNLIM),
        cost_estimate=pl.CostEstimate(flops=4 * 2 * rows * cols * depth, bytes_accessed=7 * 2**20, transcendentals=0),
        name="project_own",
    )(z, c, out_grad, out_weight, peer)


def visible(meta, seen):
    lane = lax.broadcasted_iota(jnp.int32, (8, ROWS), 1)
    prompt = jnp.zeros((8, ROWS), jnp.int32)
    own = jnp.zeros((8, ROWS), jnp.int32)
    for j in range(BLK_DEV):
        here = (lane >= j * BLK) & (lane < (j + 1) * BLK)
        resp = meta[RESP + j]
        step = lane - (j * BLK - 1)
        prompt = jnp.where(here, meta[BASE + j] + step * (1 - resp), prompt)
        own = jnp.where(here, (j * BLK + step) * resp, own)
    row = lax.broadcasted_iota(jnp.int32, (8, ROWS), 0)
    for start, limit, size in ((0, prompt - row, PKEYS), (PKEYS, own - row, ROWS)):
        for r in range(0, size, 8):
            seen[start + r : start + r + 8, :] = jnp.where(limit > r, 1.0, 0.0)


def attend_head(a, meta, q, k, v, gathered, parts, dq, dk, dv, ret, scratch):
    kc, vc, kt, qc, gc, gsum, dkc, dvc, ex, fx, dp, seen = scratch
    gsum[...] = (parts[0][...].astype(jnp.float32) + parts[1][...].astype(jnp.float32)).astype(jnp.bfloat16)
    cols = slice(a * HD, (a + 1) * HD)
    for p in range(16):
        dev, src = place(meta[PLIST + p])
        kc[p * BLK : (p + 1) * BLK, :] = gathered[dev, src, :HD]
        vc[p * BLK : (p + 1) * BLK, :] = gathered[dev, src, HD:]

    for j in range(BLK_DEV):
        src = rows_at(meta[ORDER + j])
        kc[PKEYS + j * BLK : PKEYS + (j + 1) * BLK, :] = k[src, cols]
        vc[PKEYS + j * BLK : PKEYS + (j + 1) * BLK, :] = v[src, cols]
        for h in range(2):
            to = slice(h * ROWS + j * BLK, h * ROWS + (j + 1) * BLK)
            qc[to, :] = q[src, (2 * a + h) * HD : (2 * a + h + 1) * HD]
            gc[to, :] = gsum[src, h * HD : (h + 1) * HD]
    kt[...] = kc[...].T

    blocks = [(h, half) for h in range(2) for half in range(ROWS // CHUNK)]
    count = [PKEYS // CHUNK + half + 1 for h, half in blocks]
    sums = {}

    def scores(n, c):
        h, half = blocks[n]
        rows = slice(h * ROWS + half * CHUNK, h * ROWS + (half + 1) * CHUNK)
        cut = slice(c * CHUNK, (c + 1) * CHUNK)
        raw = lax.dot_general(kc[cut, :], qc[rows, :], NT, preferred_element_type=jnp.float32)
        dprob = lax.dot_general(vc[cut, :], gc[rows, :], NT, preferred_element_type=jnp.float32)
        tanh_val = jnp.tanh(raw * (SCALE / SOFTCAP))
        expo = jnp.exp2(tanh_val * (SOFTCAP * LOG2E)) * seen[cut, half * CHUNK : (half + 1) * CHUNK]
        total, weighted = sums.get(n, (0.0, 0.0))
        total = total + jnp.sum(expo, axis=0, keepdims=True)
        weighted = weighted + jnp.sum(expo * dprob, axis=0, keepdims=True)
        sums[n] = (total, weighted)
        ex[n % 2, cut, :] = expo
        fx[n % 2, cut, :] = expo * (1.0 - tanh_val * tanh_val)
        dp[n % 2, cut, :] = dprob

    def gradients(n, c, dq_t):
        h, half = blocks[n]
        rows = slice(h * ROWS + half * CHUNK, h * ROWS + (half + 1) * CHUNK)
        cut = slice(c * CHUNK, (c + 1) * CHUNK)
        inv, delta, scaled = sums[n]
        prob16 = (ex[n % 2, cut, :] * inv).astype(jnp.bfloat16)
        dscore16 = (fx[n % 2, cut, :] * ((dp[n % 2, cut, :] - delta) * scaled)).astype(jnp.bfloat16)
        dv_part = jnp.dot(prob16, gc[rows, :], preferred_element_type=jnp.float32)
        dk_part = jnp.dot(dscore16, qc[rows, :], preferred_element_type=jnp.float32)
        if h == 0 and (half == 0 or c == PKEYS // CHUNK + 1):
            dvc[cut, :] = dv_part
            dkc[cut, :] = dk_part
        else:
            dvc[cut, :] += dv_part
            dkc[cut, :] += dk_part
        return dq_t + jnp.dot(kt[:, cut], dscore16, preferred_element_type=jnp.float32)

    for n in range(len(blocks) + 1):
        if n:
            total, weighted = sums[n - 1]
            inv = 1.0 / total
            sums[n - 1] = (inv, weighted * inv, inv * SCALE)
            dq_t = jnp.zeros((HD, CHUNK), jnp.float32)
        for c in range(KEYS // CHUNK):
            if n < len(blocks) and c < count[n]:
                scores(n, c)
            if n and c < count[n - 1]:
                dq_t = gradients(n - 1, c, dq_t)
        if n:
            h, half = blocks[n - 1]
            dq_rows = dq_t.T.astype(jnp.bfloat16)
            for j in range(CHUNK // BLK):
                dst = rows_at(meta[ORDER + half * (CHUNK // BLK) + j])
                dq[dst, h * HD : (h + 1) * HD] = dq_rows[j * BLK : (j + 1) * BLK, :]

    ret[...] = jnp.zeros(ret.shape, ret.dtype)
    for p in range(16):
        dev, dst = place(meta[PLIST + p])
        dev = DEVS - 1 - dev
        src = slice(p * BLK, (p + 1) * BLK)
        ret[dev, dst, :HD] = dkc[src, :].astype(jnp.bfloat16)
        ret[dev, dst, HD:] = dvc[src, :].astype(jnp.bfloat16)
    for j in range(BLK_DEV):
        dst = rows_at(meta[ORDER + j])
        src = slice(PKEYS + j * BLK, PKEYS + (j + 1) * BLK)
        dk[dst, cols] = dkc[src, :].astype(jnp.bfloat16)
        dv[dst, cols] = dvc[src, :].astype(jnp.bfloat16)


def attend_kernel(
    meta, q, k, v, gathered, own_a, last_a, own_b, last_b,
    dq, dk, dv, ret,
    qs, ks, vs, dqs, dks, dvs, rets, sem_in, sem_out, *scratch,
):
    loads = [(k, ks), (v, vs), (q, qs)]
    loads = [pltpu.make_async_copy(src, dst, sem_in.at[i]) for i, (src, dst) in enumerate(loads)]
    for copy in loads:
        copy.start()
    stores = [
        (rets.at[0], ret.at[:, 0]), (dqs.at[0], dq.at[:, pl.ds(0, 2 * HD)]),
        (rets.at[1], ret.at[:, 1]), (dqs.at[1], dq.at[:, pl.ds(2 * HD, 2 * HD)]), (dks, dk), (dvs, dv),
    ]
    stores = [pltpu.make_async_copy(src, dst, sem_out.at[i]) for i, (src, dst) in enumerate(stores)]
    visible(meta, scratch[-1])
    for copy in loads:
        copy.wait()
    for a in range(2):
        parts = (own_b, last_b) if a else (own_a, last_a)
        attend_head(a, meta, qs, ks, vs, gathered.at[:, a], parts, dqs.at[a], dks, dvs, rets.at[a], scratch)
        for copy in stores[2 * a : 2 + 4 * a]:
            copy.start()
    for copy in stores:
        copy.wait()


def attend(meta, queries, keys, values, gathered, parts):
    return pl.pallas_call(
        attend_kernel,
        out_shape=(
            jax.ShapeDtypeStruct(queries.shape, jnp.bfloat16),
            jax.ShapeDtypeStruct(keys.shape, jnp.bfloat16),
            jax.ShapeDtypeStruct(values.shape, jnp.bfloat16),
            jax.ShapeDtypeStruct(gathered.shape, jnp.bfloat16),
        ),
        in_specs=specs(SMEM, 1) + specs(HBM, 3) + specs(VMEM, 5),
        out_specs=tuple(specs(pl.ANY, 4)),
        scratch_shapes=[
            pltpu.VMEM(queries.shape, jnp.bfloat16),
            pltpu.VMEM(keys.shape, jnp.bfloat16),
            pltpu.VMEM(values.shape, jnp.bfloat16),
            pltpu.VMEM((2, ROWS, 2 * HD), jnp.bfloat16),
            pltpu.VMEM(keys.shape, jnp.bfloat16),
            pltpu.VMEM(values.shape, jnp.bfloat16),
            pltpu.VMEM((2, DEVS, PCAP * BLK, 2 * HD), jnp.bfloat16),
            pltpu.SemaphoreType.DMA((3,)),
            pltpu.SemaphoreType.DMA((6,)),
            pltpu.VMEM((KEYS, HD), jnp.bfloat16),
            pltpu.VMEM((KEYS, HD), jnp.bfloat16),
            pltpu.VMEM((HD, KEYS), jnp.bfloat16),
            pltpu.VMEM((2 * ROWS, HD), jnp.bfloat16),
            pltpu.VMEM((2 * ROWS, HD), jnp.bfloat16),
            pltpu.VMEM((ROWS, 2 * HD), jnp.bfloat16),
            pltpu.VMEM((KEYS, HD), jnp.float32),
            pltpu.VMEM((KEYS, HD), jnp.float32),
            pltpu.VMEM((2, KEYS, CHUNK), jnp.float32),
            pltpu.VMEM((2, KEYS, CHUNK), jnp.float32),
            pltpu.VMEM((2, KEYS, CHUNK), jnp.float32),
            pltpu.VMEM((KEYS, ROWS), jnp.float32),
        ],
        compiler_params=params(32),
        cost_estimate=pl.CostEstimate(flops=4 * 10**9, bytes_accessed=8 * 2**20, transcendentals=6 * 10**6),
        name="attend",
    )(meta, queries, keys, values, gathered, *parts)


def finish_kernel(meta, own_k, own_v, ret, dk, dv):
    for i, (own, out) in enumerate(((own_k, dk), (own_v, dv))):
        out[...] = own[...]
        for r in range(PCAP):

            @pl.when(meta[COUNT] > r)
            def _(r=r, i=i, out=out):
                rows = slice(r * BLK, (r + 1) * BLK)
                for a in range(2):
                    total = ret[0, a, rows, i * HD : (i + 1) * HD].astype(jnp.float32)
                    for d in range(1, DEVS):
                        total = total + ret[d, a, rows, i * HD : (i + 1) * HD].astype(jnp.float32)
                    at = rows_at(meta[ORDER + BLK_DEV - 1 - r])
                    out[at, a * HD : (a + 1) * HD] = total.astype(jnp.bfloat16)


def finish(meta, own_k, own_v, ret):
    out = jax.ShapeDtypeStruct(own_k.shape, jnp.bfloat16)
    return pl.pallas_call(
        finish_kernel,
        out_shape=(out, out),
        in_specs=specs(SMEM, 1) + specs(VMEM, 3),
        out_specs=tuple(specs(VMEM, 2)),
        compiler_params=params(8),
        name="finish",
    )(meta, own_k, own_v, ret)


def scalar(axis):
    return lax.axis_index(axis).astype(jnp.int32).reshape(1)


def shards(out_grad, out_weight, query_states, key_states, value_states, slot_seq, slot_pos, fork_depth):
    here, z, c = scalar("seq"), scalar("mp"), scalar("section")
    pair_a = [(i, i ^ 1) for i in range(4)]
    pair_b = [(i, 3 - i) for i in range(4)]
    out_grad, out_weight = out_grad.T, out_weight.T

    slots = (slot_seq, slot_pos, fork_depth)
    peer, meta, prompt = project_peer(z, c, here, out_grad, out_weight, *slots, key_states, value_states)
    peer = lax.ppermute(peer, "section", [(0, 1), (1, 0)])
    gathered = lax.all_to_all(prompt, "seq", 0, 0, tiled=True)
    send_a, keep_a, send_b, keep_b = project_own(z, c, out_grad, out_weight, peer)
    recv_a = lax.ppermute(send_a, "mp", pair_a)
    recv_b = lax.ppermute(send_b, "mp", pair_b)
    next_a = (keep_a[1].astype(jnp.float32) + recv_a[1].astype(jnp.float32)).astype(jnp.bfloat16)
    next_b = (keep_b[1].astype(jnp.float32) + recv_b[1].astype(jnp.float32)).astype(jnp.bfloat16)
    keep_a, recv_a, keep_b, recv_b, next_a, next_b = lax.optimization_barrier(
        (keep_a, recv_a, keep_b, recv_b, next_a, next_b)
    )
    own_a = (keep_a[0].astype(jnp.float32) + recv_a[0].astype(jnp.float32)).astype(jnp.bfloat16)
    own_b = (keep_b[0].astype(jnp.float32) + recv_b[0].astype(jnp.float32)).astype(jnp.bfloat16)
    last_a = lax.ppermute(next_a, "mp", pair_b)
    last_b = lax.ppermute(next_b, "mp", pair_a)
    parts = (own_a, last_a, own_b, last_b)
    dq, own_k, own_v, ret = attend(meta, query_states, key_states, value_states, gathered, parts)
    ret = lax.all_to_all(ret, "seq", 0, 0, tiled=True, axis_index_groups=[list(BACK)])
    dk, dv = finish(meta, own_k, own_v, ret)
    return dq, dk, dv


def solution(mesh):
    wide = P("seq", ("mp", "section"))
    return jax.shard_map(
        shards,
        mesh=mesh,
        in_specs=(wide, P(None, ("mp", "section")), wide, wide, wide, P(), P(), P()),
        out_specs=(wide, wide, wide),
        check_vma=False,
    )
```

```python
import jax
import jax.numpy as jnp
from jax import lax
from jax.experimental import pallas as pl
from jax.experimental.pallas import tpu as pltpu
from jax.sharding import PartitionSpec as P

HD = 128
BLK = 64
BLK_DEV = 8
PCAP = 2
DEVS = 16
ROWS = BLK * BLK_DEV
PKEYS = 16 * BLK
KEYS = PKEYS + ROWS
CHUNK = 256

SCALE = 144.0 ** (-0.5)
SOFTCAP = 50.0
LOG2E = 1.4426950408889634

PLIST = 0
ORDER = 16
BASE = 24
RESP = 32
COUNT = 40
SPARE = 41
META = 48

LIM = 60
OWNLIM = 60

SMEM = pltpu.MemorySpace.SMEM
VMEM = pltpu.MemorySpace.VMEM
HBM = pltpu.MemorySpace.HBM
NT = (((1,), (1,)), ((), ()))
TN = (((0,), (0,)), ((), ()))


def params(mib):
    return pltpu.CompilerParams(vmem_limit_bytes=mib * 2**20)


def specs(space, n):
    return [pl.BlockSpec(memory_space=space)] * n


def rows_at(i):
    return pl.ds(pl.multiple_of(i * BLK, BLK), BLK)


def place(slot):
    return lax.shift_right_logical(slot, 1), rows_at(slot & 1)


KEYS_ORDER, BACK_ORDER = 0, 10


def make_layout(here, seq, pos, depth, keys, values, meta, block):
    me = here[0]

    for dev in range(DEVS):
        count = jnp.int32(0)
        for b in range(BLK_DEV):
            slot = dev * BLK_DEV + b
            prompt = seq[slot] == 0
            at = jnp.where(prompt, PLIST + pos[slot], SPARE)
            meta[at] = dev * PCAP + jnp.minimum(count, PCAP - 1)
            count = count + prompt.astype(jnp.int32)

    count = jnp.int32(0)
    block[...] = jnp.zeros(block.shape, block.dtype)
    for b in range(BLK_DEV):
        slot = me * BLK_DEV + b
        prompt = seq[slot] == 0
        at = jnp.where(prompt, BLK_DEV - 1 - count, pos[slot])
        meta[ORDER + at] = jnp.int32(b)
        meta[RESP + at] = 1 - prompt.astype(jnp.int32)
        meta[BASE + at] = jnp.where(prompt, pos[slot], depth[jnp.maximum(seq[slot] - 1, 0)]) * BLK

        @pl.when(prompt)
        def _(count=count, b=b):
            rows = rows_at(jnp.minimum(count, PCAP - 1))
            for a in range(2):
                block[a, rows, :HD] = keys[b * BLK : (b + 1) * BLK, a * HD : (a + 1) * HD]
                block[a, rows, HD:] = values[b * BLK : (b + 1) * BLK, a * HD : (a + 1) * HD]

        count = count + prompt.astype(jnp.int32)
    meta[COUNT] = count


def target(z, r):
    z = z[0]
    return jnp.where(r == 0, (3 - z) ^ 1, jnp.where(r == 1, z ^ 1, jnp.where(r == 2, 3 - z, z)))


def project_peer_kernel(z, c, here, grad, weight, seq, pos, depth, keys, values, out, meta, prompt, block, sems):
    r = pl.program_id(0)
    copies = [pltpu.make_async_copy(block, prompt.at[d], sems.at[d]) for d in range(DEVS)]

    def product():
        out[0] = lax.dot_general(grad[...], weight[...], TN, preferred_element_type=jnp.float32).astype(jnp.bfloat16)

    @pl.when(r == 0)
    def _():
        make_layout(here, seq, pos, depth, keys, values, meta, block)
        for copy in copies:
            copy.start()
        product()

    @pl.when(r > 0)
    def _():
        product()

    @pl.when(r == 3)
    def _():
        for copy in copies:
            copy.wait()


def project_peer(z, c, here, out_grad, out_weight, slot_seq, slot_pos, fork_depth, keys, values):
    depth, rows = out_grad.shape
    cols = out_weight.shape[1] // 8
    block = (2, PCAP * BLK, 2 * HD)
    return pl.pallas_call(
        project_peer_kernel,
        out_shape=(
            jax.ShapeDtypeStruct((4, rows, cols), jnp.bfloat16),
            jax.ShapeDtypeStruct((META,), jnp.int32),
            jax.ShapeDtypeStruct((DEVS, *block), jnp.bfloat16),
        ),
        grid_spec=pltpu.PrefetchScalarGridSpec(
            num_scalar_prefetch=3,
            grid=(4,),
            in_specs=[
                pl.BlockSpec((depth, rows), lambda r, z, c, here: (0, 0)),
                pl.BlockSpec((depth, cols), lambda r, z, c, here: (0, target(z, r) * 2 + 1 - c[0])),
                *specs(SMEM, 3),
                pl.BlockSpec(keys.shape, lambda r, z, c, here: (0, 0)),
                pl.BlockSpec(values.shape, lambda r, z, c, here: (0, 0)),
            ],
            out_specs=(
                pl.BlockSpec((1, rows, cols), lambda r, z, c, here: (r, 0, 0)),
                pl.BlockSpec(memory_space=SMEM),
                pl.BlockSpec(memory_space=pl.ANY),
            ),
            scratch_shapes=[pltpu.VMEM(block, jnp.bfloat16), pltpu.SemaphoreType.DMA((DEVS,))],
        ),
        compiler_params=params(LIM),
        cost_estimate=pl.CostEstimate(flops=4 * 2 * rows * cols * depth, bytes_accessed=5 * 2**20, transcendentals=0),
        name="project_peer",
    )(z, c, here, out_grad, out_weight, slot_seq, slot_pos, fork_depth, keys, values)


def project_own_kernel(z, c, grad, weight, peer, send_a, keep_a, send_b, keep_b):
    r = pl.program_id(0)
    both = lax.dot_general(grad[...], weight[...], TN, preferred_element_type=jnp.float32)
    both = (both + peer[0].astype(jnp.float32)).astype(jnp.bfloat16)
    half = both.shape[1] // 2
    first, second = both[:, :half], both[:, half:]

    @pl.when(r < 2)
    def _():
        send_a[0] = first

    @pl.when(r >= 2)
    def _():
        keep_a[0] = first

    @pl.when(r % 2 == 0)
    def _():
        send_b[0] = second

    @pl.when(r % 2 == 1)
    def _():
        keep_b[0] = second


def project_own(z, c, out_grad, out_weight, peer):
    depth, rows = out_grad.shape
    cols = out_weight.shape[1] // 8
    part = jax.ShapeDtypeStruct((2, rows, cols // 2), jnp.bfloat16)

    def at(index):
        return pl.BlockSpec((1, rows, cols // 2), lambda r, z, c: (index(r), 0, 0))

    return pl.pallas_call(
        project_own_kernel,
        out_shape=(part, part, part, part),
        grid_spec=pltpu.PrefetchScalarGridSpec(
            num_scalar_prefetch=2,
            grid=(4,),
            in_specs=[
                pl.BlockSpec((depth, rows), lambda r, z, c: (0, 0)),
                pl.BlockSpec((depth, cols), lambda r, z, c: (0, target(z, r) * 2 + c[0])),
                pl.BlockSpec((1, rows, cols), lambda r, z, c: (r, 0, 0)),
            ],
            out_specs=(
                at(lambda r: jnp.where(r == 0, 1, 0)),
                at(lambda r: jnp.where(r == 3, 0, 1)),
                at(lambda r: jnp.where(r == 0, 1, 0)),
                at(lambda r: jnp.where(r >= 2, 0, 1)),
            ),
        ),
        compiler_params=params(OWNLIM),
        cost_estimate=pl.CostEstimate(flops=4 * 2 * rows * cols * depth, bytes_accessed=7 * 2**20, transcendentals=0),
        name="project_own",
    )(z, c, out_grad, out_weight, peer)


def visible(meta, seen):
    lane = lax.broadcasted_iota(jnp.int32, (8, ROWS), 1)
    prompt = jnp.zeros((8, ROWS), jnp.int32)
    own = jnp.zeros((8, ROWS), jnp.int32)
    for j in range(BLK_DEV):
        here = (lane >= j * BLK) & (lane < (j + 1) * BLK)
        resp = meta[RESP + j]
        step = lane - (j * BLK - 1)
        prompt = jnp.where(here, meta[BASE + j] + step * (1 - resp), prompt)
        own = jnp.where(here, (j * BLK + step) * resp, own)
    row = lax.broadcasted_iota(jnp.int32, (8, ROWS), 0)
    for start, limit, size in ((0, prompt - row, PKEYS), (PKEYS, own - row, ROWS)):
        for r in range(0, size, 8):
            seen[start + r : start + r + 8, :] = jnp.where(limit > r, 1.0, 0.0)


def attend_head(a, meta, q, k, v, gathered, parts, dq, dk, dv, ret, scratch):
    kc, vc, kt, qc, gc, gsum, dkc, dvc, ex, fx, dp, seen = scratch
    gsum[...] = (parts[0][...].astype(jnp.float32) + parts[1][...].astype(jnp.float32)).astype(jnp.bfloat16)
    cols = slice(a * HD, (a + 1) * HD)
    for p in range(16):
        dev, src = place(meta[PLIST + p])
        dev = dev ^ KEYS_ORDER
        kc[p * BLK : (p + 1) * BLK, :] = gathered[dev, src, :HD]
        vc[p * BLK : (p + 1) * BLK, :] = gathered[dev, src, HD:]

    for j in range(BLK_DEV):
        src = rows_at(meta[ORDER + j])
        kc[PKEYS + j * BLK : PKEYS + (j + 1) * BLK, :] = k[src, cols]
        vc[PKEYS + j * BLK : PKEYS + (j + 1) * BLK, :] = v[src, cols]
        for h in range(2):
            to = slice(h * ROWS + j * BLK, h * ROWS + (j + 1) * BLK)
            qc[to, :] = q[src, (2 * a + h) * HD : (2 * a + h + 1) * HD]
            gc[to, :] = gsum[src, h * HD : (h + 1) * HD]
    kt[...] = kc[...].T

    blocks = [(h, half) for h in range(2) for half in range(ROWS // CHUNK)]
    count = [PKEYS // CHUNK + half + 1 for h, half in blocks]
    sums = {}

    def scores(n, c):
        h, half = blocks[n]
        rows = slice(h * ROWS + half * CHUNK, h * ROWS + (half + 1) * CHUNK)
        cut = slice(c * CHUNK, (c + 1) * CHUNK)
        raw = lax.dot_general(kc[cut, :], qc[rows, :], NT, preferred_element_type=jnp.float32)
        dprob = lax.dot_general(vc[cut, :], gc[rows, :], NT, preferred_element_type=jnp.float32)
        tanh_val = jnp.tanh(raw * (SCALE / SOFTCAP))
        expo = jnp.exp2(tanh_val * (SOFTCAP * LOG2E)) * seen[cut, half * CHUNK : (half + 1) * CHUNK]
        total, weighted = sums.get(n, (0.0, 0.0))
        total = total + jnp.sum(expo, axis=0, keepdims=True)
        weighted = weighted + jnp.sum(expo * dprob, axis=0, keepdims=True)
        sums[n] = (total, weighted)
        ex[n % 2, cut, :] = expo
        fx[n % 2, cut, :] = expo * (1.0 - tanh_val * tanh_val)
        dp[n % 2, cut, :] = dprob

    def gradients(n, c, dq_t):
        h, half = blocks[n]
        rows = slice(h * ROWS + half * CHUNK, h * ROWS + (half + 1) * CHUNK)
        cut = slice(c * CHUNK, (c + 1) * CHUNK)
        inv, delta, scaled = sums[n]
        prob16 = (ex[n % 2, cut, :] * inv).astype(jnp.bfloat16)
        dscore16 = (fx[n % 2, cut, :] * ((dp[n % 2, cut, :] - delta) * scaled)).astype(jnp.bfloat16)
        dv_part = jnp.dot(prob16, gc[rows, :], preferred_element_type=jnp.float32)
        dk_part = jnp.dot(dscore16, qc[rows, :], preferred_element_type=jnp.float32)
        if h == 0 and (half == 0 or c == PKEYS // CHUNK + 1):
            dvc[cut, :] = dv_part
            dkc[cut, :] = dk_part
        else:
            dvc[cut, :] += dv_part
            dkc[cut, :] += dk_part
        return dq_t + jnp.dot(kt[:, cut], dscore16, preferred_element_type=jnp.float32)

    for n in range(len(blocks) + 1):
        if n:
            total, weighted = sums[n - 1]
            inv = 1.0 / total
            sums[n - 1] = (inv, weighted * inv, inv * SCALE)
            dq_t = jnp.zeros((HD, CHUNK), jnp.float32)
        for c in range(KEYS // CHUNK):
            if n < len(blocks) and c < count[n]:
                scores(n, c)
            if n and c < count[n - 1]:
                dq_t = gradients(n - 1, c, dq_t)
        if n:
            h, half = blocks[n - 1]
            dq_rows = dq_t.T.astype(jnp.bfloat16)
            for j in range(CHUNK // BLK):
                dst = rows_at(meta[ORDER + half * (CHUNK // BLK) + j])
                dq[dst, h * HD : (h + 1) * HD] = dq_rows[j * BLK : (j + 1) * BLK, :]

    ret[...] = jnp.zeros(ret.shape, ret.dtype)
    for p in range(16):
        dev, dst = place(meta[PLIST + p])
        dev = dev ^ BACK_ORDER
        src = slice(p * BLK, (p + 1) * BLK)
        ret[dev, dst, :HD] = dkc[src, :].astype(jnp.bfloat16)
        ret[dev, dst, HD:] = dvc[src, :].astype(jnp.bfloat16)
    for j in range(BLK_DEV):
        dst = rows_at(meta[ORDER + j])
        src = slice(PKEYS + j * BLK, PKEYS + (j + 1) * BLK)
        dk[dst, cols] = dkc[src, :].astype(jnp.bfloat16)
        dv[dst, cols] = dvc[src, :].astype(jnp.bfloat16)


def attend_kernel(
    meta, q, k, v, gathered, own_a, last_a, own_b, last_b,
    dq, dk, dv, ret,
    qs, ks, vs, dqs, dks, dvs, rets, sem_in, sem_out, *scratch,
):
    loads = [(k, ks), (v, vs), (q, qs)]
    loads = [pltpu.make_async_copy(src, dst, sem_in.at[i]) for i, (src, dst) in enumerate(loads)]
    for copy in loads:
        copy.start()
    stores = [
        (rets.at[0], ret.at[:, 0]), (dqs.at[0], dq.at[:, pl.ds(0, 2 * HD)]),
        (rets.at[1], ret.at[:, 1]), (dqs.at[1], dq.at[:, pl.ds(2 * HD, 2 * HD)]), (dks, dk), (dvs, dv),
    ]
    stores = [pltpu.make_async_copy(src, dst, sem_out.at[i]) for i, (src, dst) in enumerate(stores)]
    visible(meta, scratch[-1])
    for copy in loads:
        copy.wait()
    for a in range(2):
        parts = (own_b, last_b) if a else (own_a, last_a)
        attend_head(a, meta, qs, ks, vs, gathered.at[:, a], parts, dqs.at[a], dks, dvs, rets.at[a], scratch)
        for copy in stores[2 * a : 2 + 4 * a]:
            copy.start()
    for copy in stores:
        copy.wait()


def attend(meta, queries, keys, values, gathered, parts):
    return pl.pallas_call(
        attend_kernel,
        out_shape=(
            jax.ShapeDtypeStruct(queries.shape, jnp.bfloat16),
            jax.ShapeDtypeStruct(keys.shape, jnp.bfloat16),
            jax.ShapeDtypeStruct(values.shape, jnp.bfloat16),
            jax.ShapeDtypeStruct(gathered.shape, jnp.bfloat16),
        ),
        in_specs=specs(SMEM, 1) + specs(HBM, 3) + specs(VMEM, 5),
        out_specs=tuple(specs(pl.ANY, 4)),
        scratch_shapes=[
            pltpu.VMEM(queries.shape, jnp.bfloat16),
            pltpu.VMEM(keys.shape, jnp.bfloat16),
            pltpu.VMEM(values.shape, jnp.bfloat16),
            pltpu.VMEM((2, ROWS, 2 * HD), jnp.bfloat16),
            pltpu.VMEM(keys.shape, jnp.bfloat16),
            pltpu.VMEM(values.shape, jnp.bfloat16),
            pltpu.VMEM((2, DEVS, PCAP * BLK, 2 * HD), jnp.bfloat16),
            pltpu.SemaphoreType.DMA((3,)),
            pltpu.SemaphoreType.DMA((6,)),
            pltpu.VMEM((KEYS, HD), jnp.bfloat16),
            pltpu.VMEM((KEYS, HD), jnp.bfloat16),
            pltpu.VMEM((HD, KEYS), jnp.bfloat16),
            pltpu.VMEM((2 * ROWS, HD), jnp.bfloat16),
            pltpu.VMEM((2 * ROWS, HD), jnp.bfloat16),
            pltpu.VMEM((ROWS, 2 * HD), jnp.bfloat16),
            pltpu.VMEM((KEYS, HD), jnp.float32),
            pltpu.VMEM((KEYS, HD), jnp.float32),
            pltpu.VMEM((2, KEYS, CHUNK), jnp.float32),
            pltpu.VMEM((2, KEYS, CHUNK), jnp.float32),
            pltpu.VMEM((2, KEYS, CHUNK), jnp.float32),
            pltpu.VMEM((KEYS, ROWS), jnp.float32),
        ],
        compiler_params=params(32),
        cost_estimate=pl.CostEstimate(flops=4 * 10**9, bytes_accessed=8 * 2**20, transcendentals=6 * 10**6),
        name="attend",
    )(meta, queries, keys, values, gathered, *parts)


def finish_kernel(meta, own_k, own_v, ret, dk, dv):
    for i, (own, out) in enumerate(((own_k, dk), (own_v, dv))):
        out[...] = own[...]
        for r in range(PCAP):

            @pl.when(meta[COUNT] > r)
            def _(r=r, i=i, out=out):
                rows = slice(r * BLK, (r + 1) * BLK)
                for a in range(2):
                    total = ret[0, a, rows, i * HD : (i + 1) * HD].astype(jnp.float32)
                    for d in range(1, DEVS):
                        total = total + ret[d, a, rows, i * HD : (i + 1) * HD].astype(jnp.float32)
                    at = rows_at(meta[ORDER + BLK_DEV - 1 - r])
                    out[at, a * HD : (a + 1) * HD] = total.astype(jnp.bfloat16)


def finish(meta, own_k, own_v, ret):
    out = jax.ShapeDtypeStruct(own_k.shape, jnp.bfloat16)
    return pl.pallas_call(
        finish_kernel,
        out_shape=(out, out),
        in_specs=specs(SMEM, 1) + specs(VMEM, 3),
        out_specs=tuple(specs(VMEM, 2)),
        compiler_params=params(8),
        name="finish",
    )(meta, own_k, own_v, ret)


def scalar(axis):
    return lax.axis_index(axis).astype(jnp.int32).reshape(1)


def shards(out_grad, out_weight, query_states, key_states, value_states, slot_seq, slot_pos, fork_depth):
    here, z, c = scalar("seq"), scalar("mp"), scalar("section")
    pair_a = [(i, i ^ 1) for i in range(4)]
    pair_b = [(i, 3 - i) for i in range(4)]
    out_grad, out_weight = out_grad.T, out_weight.T

    slots = (slot_seq, slot_pos, fork_depth)
    peer, meta, prompt = project_peer(z, c, here, out_grad, out_weight, *slots, key_states, value_states)
    peer = lax.ppermute(peer, "section", [(0, 1), (1, 0)])
    gathered = lax.all_to_all(prompt, "seq", 0, 0, tiled=True, axis_index_groups=[[i ^ KEYS_ORDER for i in range(DEVS)]])
    send_a, keep_a, send_b, keep_b = project_own(z, c, out_grad, out_weight, peer)
    recv_a = lax.ppermute(send_a, "mp", pair_a)
    recv_b = lax.ppermute(send_b, "mp", pair_b)
    next_a = (keep_a[1].astype(jnp.float32) + recv_a[1].astype(jnp.float32)).astype(jnp.bfloat16)
    next_b = (keep_b[1].astype(jnp.float32) + recv_b[1].astype(jnp.float32)).astype(jnp.bfloat16)
    keep_a, recv_a, keep_b, recv_b, next_a, next_b = lax.optimization_barrier(
        (keep_a, recv_a, keep_b, recv_b, next_a, next_b)
    )
    own_a = (keep_a[0].astype(jnp.float32) + recv_a[0].astype(jnp.float32)).astype(jnp.bfloat16)
    own_b = (keep_b[0].astype(jnp.float32) + recv_b[0].astype(jnp.float32)).astype(jnp.bfloat16)
    last_a = lax.ppermute(next_a, "mp", pair_b)
    last_b = lax.ppermute(next_b, "mp", pair_a)
    parts = (own_a, last_a, own_b, last_b)
    dq, own_k, own_v, ret = attend(meta, query_states, key_states, value_states, gathered, parts)
    ret = lax.all_to_all(ret, "seq", 0, 0, tiled=True, axis_index_groups=[[i ^ BACK_ORDER for i in range(DEVS)]])
    dk, dv = finish(meta, own_k, own_v, ret)
    return dq, dk, dv


def solution(mesh):
    wide = P("seq", ("mp", "section"))
    return jax.shard_map(
        shards,
        mesh=mesh,
        in_specs=(wide, P(None, ("mp", "section")), wide, wide, wide, P(), P(), P()),
        out_specs=(wide, wide, wide),
        check_vma=False,
    )
```
